256 devices in a mesh: region: 32 (over z, x), slot: 8 (over y, core).
Axes of the slice: x: 4, y: 4, z: 8, core: 2. Of those that a mesh axis runs over, the one named last changes fastest.
Arguments:
- flux: float32 [8, 1048576], P('slot', 'region'), may hold values from -6 to 6
- prior_flux: float32 [8, 1048576], P('slot', 'region'), may hold values from -6 to 6
- prior_precision: float32 [8, 1048576], P('slot', 'region'), may hold values from 0.2 to 2
- obs_value: float32 [524288], P('region'), may hold values from -10 to 10
- obs_weight: float32 [524288], P('region'), may hold values from 0.25 to 4
- footprint: float32 [8, 32, 32, 8, 4096], P('slot', 'region'), may hold values from -0.25 to 0.25
- counts: int32 [8, 32, 32], P('slot', 'region'), may hold values from 1 to 8, as said below
- obs_blocks: int32 [8, 32, 32, 8], P('slot', 'region'), may hold values from 0 to 255
- cell_blocks: int32 [8, 32, 32, 8], P('slot', 'region'), may hold values from 0 to 511
Outputs:
- increment: float32 [8, 1048576], P('slot', 'region')
- gradient: float32 [8, 1048576], P('slot', 'region')
The draws below stay inside these ranges and needn't reach their ends.
Inputs may be any that keep to these rules, and one draw needn't show every extreme that they name: `counts`: in every slot some owner region receives 8 live blocks from every source region.
All inputs are finite; a program needn't handle non-finite values.
Results may differ from the reference program's by a relative error of at most 0.00026.
Values sent between devices are 32-bit elements; how exact they have to be, the bound alone decides.
A program may use at most 64 MiB of HBM per device.

```python
import math
import jax
import jax.numpy as jnp
from jax import lax

BLOCK = 64
SLOTS = 8
ITERS = 2
MOST = 8
REGIONS = 32
CELLS = 1048576
OBS = 524288
CBLK = 512
OBLK = 256


def draw_counts(key, part):
    key = jax.random.fold_in(key, 7)
    first, second = jax.random.split(key)
    base = jax.random.randint(first, (SLOTS, REGIONS, REGIONS), 1, MOST + 1)
    busiest = jax.random.randint(second, (SLOTS, 1, 1), 0, REGIONS)
    column = lax.broadcasted_iota(jnp.int32, (SLOTS, REGIONS, REGIONS), 2)
    return jnp.where(column == busiest, MOST, base).astype(jnp.int32)


def plant(array, own_key, smallest, high):
    place = [jax.random.randint(jax.random.fold_in(own_key, axis), (), 0, length) for axis, length in enumerate(array.shape)]
    longest = array.shape.index(max(array.shape))
    beside = place[:longest] + [(place[longest] + 1) % array.shape[longest]] + place[longest + 1:]
    return array.at[tuple(place)].set(smallest).at[tuple(beside)].set(high)


def shard_levels(own_key, dims, shards, low, largest):
    def one(axis_at, shards_of):
        heights = jax.random.uniform(jax.random.fold_in(jax.random.fold_in(own_key, 6), axis_at), (shards_of,), jnp.float32, low / len(shards), largest / len(shards))
        return jnp.repeat(jnp.exp(heights), dims[axis_at] // shards_of).reshape((-1,) + (1,) * (len(dims) - axis_at - 1))

    gain = one(*shards[0])
    for cut in shards[1:]:
        gain = gain * one(*cut)
    return gain


def scatter_about(own_key, dims, width, most, pieces=(), held_as=jnp.bfloat16):
    loudness = shard_levels(own_key, dims, pieces, -0.22, 0.18) if pieces else 1.0
    drawn = jax.random.normal(own_key, dims, jnp.float32) * width * loudness
    return jnp.minimum(jnp.maximum(drawn, -most), most).astype(held_as)


def setup_inputs(seed: int = 0) -> dict:
    arg_keys = jax.random.split(jax.random.key(seed), 10)
    flux = scatter_about(arg_keys[0], (SLOTS, CELLS), 1.0, 6.0, ((0, 8), (1, 32)), jnp.float32)
    prior_flux = scatter_about(arg_keys[1], (SLOTS, CELLS), 1.0, 6.0, ((0, 8), (1, 32)), jnp.float32)
    prior_precision = jnp.clip(jnp.exp(math.log(2.0) - 2.3025851 * jax.random.uniform(arg_keys[2], (SLOTS, CELLS), jnp.float32) ** shard_levels(arg_keys[2], (SLOTS, CELLS), ((0, 8), (1, 32)), -0.2, 0.2)), 0.2, 2.0)
    obs_value = scatter_about(arg_keys[3], (OBS,), 2.0, 10.0, ((0, 32),), jnp.float32)
    obs_weight = jnp.clip(jnp.exp(math.log(4.0) - 2.7725887 * jax.random.uniform(arg_keys[4], (OBS,), jnp.float32) ** shard_levels(arg_keys[4], (OBS,), ((0, 32),), -0.2, 0.2)), 0.25, 4.0)
    footprint = scatter_about(arg_keys[5], (SLOTS, REGIONS, REGIONS, MOST, BLOCK * BLOCK), (BLOCK * MOST) ** -0.5, 0.25, ((0, 8), (1, 32)), jnp.float32)
    counts = draw_counts(jax.random.fold_in(arg_keys[9], 71), 0)
    obs_blocks = plant(jax.random.randint(arg_keys[7], (SLOTS, REGIONS, REGIONS, MOST), 0, OBLK), jax.random.fold_in(arg_keys[7], 1), 0, OBLK - 1).astype(jnp.int32)
    cell_blocks = plant(jax.random.randint(arg_keys[8], (SLOTS, REGIONS, REGIONS, MOST), 0, CBLK), jax.random.fold_in(arg_keys[8], 1), 0, CBLK - 1).astype(jnp.int32)
    return {"flux": flux, "prior_flux": prior_flux, "prior_precision": prior_precision, "obs_value": obs_value, "obs_weight": obs_weight, "footprint": footprint, "counts": counts, "obs_blocks": obs_blocks, "cell_blocks": cell_blocks}


def live_mask(counts):
    slots = lax.broadcasted_iota(jnp.int32, counts.shape + (MOST,), 3)
    return (slots < counts[..., None]).astype(jnp.float32)


def forward(field, footprint, valid, obs_blocks, cell_blocks):
    rows = field.reshape(SLOTS, REGIONS * CBLK, BLOCK)
    source = lax.broadcasted_iota(jnp.int32, (REGIONS, REGIONS, MOST), 0)
    owner = lax.broadcasted_iota(jnp.int32, (REGIONS, REGIONS, MOST), 1)

    def one_slot(slot):
        blocks = footprint[slot].reshape(REGIONS, REGIONS, MOST, BLOCK, BLOCK)
        picked = rows[slot][source * CBLK + cell_blocks[slot]]
        part = jnp.einsum("qpkoc,qpkc->qpko", blocks, picked, precision=lax.Precision.HIGHEST)
        part = part * valid[slot][..., None]
        target = (owner * OBLK + obs_blocks[slot]).reshape(-1)
        return jax.ops.segment_sum(part.reshape(-1, BLOCK), target, REGIONS * OBLK)

    total = jnp.sum(lax.map(one_slot, jnp.arange(SLOTS, dtype=jnp.int32)), axis=0)
    return total.reshape(OBS)


def adjoint(values, footprint, valid, obs_blocks, cell_blocks):
    rows = values.reshape(REGIONS * OBLK, BLOCK)
    source = lax.broadcasted_iota(jnp.int32, (REGIONS, REGIONS, MOST), 0)
    owner = lax.broadcasted_iota(jnp.int32, (REGIONS, REGIONS, MOST), 1)

    def one_slot(slot):
        blocks = footprint[slot].reshape(REGIONS, REGIONS, MOST, BLOCK, BLOCK)
        picked = rows[owner * OBLK + obs_blocks[slot]]
        term = jnp.einsum("qpkoc,qpko->qpkc", blocks, picked, precision=lax.Precision.HIGHEST)
        term = term * valid[slot][..., None]
        target = (source * CBLK + cell_blocks[slot]).reshape(-1)
        return jax.ops.segment_sum(term.reshape(-1, BLOCK), target, REGIONS * CBLK).reshape(CELLS)

    return lax.map(one_slot, jnp.arange(SLOTS, dtype=jnp.int32))


def reference(flux, prior_flux, prior_precision, obs_value, obs_weight, footprint, counts, obs_blocks, cell_blocks):
    valid = live_mask(counts)
    state = flux
    increment = jnp.zeros_like(flux)
    gradient = jnp.zeros_like(flux)
    for step in range(ITERS):
        predicted = forward(state, footprint, valid, obs_blocks, cell_blocks)
        weighted = obs_weight * (predicted - obs_value)
        gradient = adjoint(weighted, footprint, valid, obs_blocks, cell_blocks) + prior_precision * (state - prior_flux)
        image = forward(gradient, footprint, valid, obs_blocks, cell_blocks)
        numer = jnp.sum(gradient * gradient)
        denom = jnp.sum(obs_weight * image * image) + jnp.sum(prior_precision * gradient * gradient)
        alpha = numer / denom
        state = state - alpha * gradient
        increment = increment - alpha * gradient
    return increment, gradient
```

```python
import jax
import jax.numpy as jnp
from jax import lax
from jax.experimental import pallas as pl
from jax.experimental.pallas import tpu as pltpu
from jax.sharding import PartitionSpec as P

REGIONS = 32
SLOTS = 8
MOST = 8
BLOCK = 64
BLOCKS = REGIONS * MOST
CBLK = 512
LANES = 128
CHUNKS = 8
CHUNK_LANES = BLOCK * BLOCK // CHUNKS
MESH = pl.DeviceIdType.MESH
F32 = jnp.float32
BF16 = jnp.bfloat16

INDEX, FWD0, BACK0, FWD1, BACK1, FWD2, SUM0, SUM1, SUM2, GATHER0, GATHER1, LAST_SLOT, LAST_REGION = range(13)
EXCHANGES = 13


def iota(shape, axis):
    return lax.broadcasted_iota(jnp.int32, shape, axis)


def lane_region(lane):
    return (lane % LANES) // 4


def lane_place(lane):
    return (lane // LANES) * 4 + lane % 4


def pick(x, onehot, dims):
    high = x.astype(BF16)
    rest = x - high.astype(F32)
    middle = rest.astype(BF16)
    low = (rest - middle.astype(F32)).astype(BF16)
    pieces = jnp.concatenate([high, middle, low], axis=0)
    out = lax.dot_general(pieces, onehot, (dims, ((), ())), preferred_element_type=F32)
    return out[:BLOCK] + out[BLOCK : 2 * BLOCK] + out[2 * BLOCK :]


AS_IS = ((1,), (0,))
TURNED = ((1,), (1,))


def to_rows(x):
    return jnp.concatenate([x[:, :LANES], x[:, LANES:]], axis=0).T


def from_rows(x):
    y = x.T
    return jnp.concatenate([y[:BLOCK], y[BLOCK:]], axis=1)


def load_cells(ref):
    x = ref[...]
    a, b = x[:LANES].T, x[LANES:].T
    return jnp.concatenate([a[:BLOCK], b[:BLOCK], a[BLOCK:], b[BLOCK:]], axis=1)


def store_cells(x):
    a = jnp.concatenate([x[:, :LANES], x[:, 2 * LANES : 3 * LANES]], axis=0).T
    b = jnp.concatenate([x[:, LANES : 2 * LANES], x[:, 3 * LANES :]], axis=0).T
    return jnp.concatenate([a, b], axis=0)


def total(x):
    return jnp.sum(jnp.sum(x, axis=0, keepdims=True), axis=1, keepdims=True)


def kernel(
    flux, prior, precision, value, weight, foot, counts, obs_blocks, cell_blocks,
    increment, gradient,
    foot_in, foot_t, picked, part, cells, onehot_c, onehot_a, index_out, index_in,
    fwd_out, fwd_in, back_out, back_in, last_back_out, last_back_in,
    dense, sums, spread, last_spread, spread_out, last_spread_out,
    slot_out, slot_in, region_out, region_in,
    foot_sem, send_sem, recv_sem,
):
    me = lax.axis_index("region")
    slot = lax.axis_index("slot")

    def each(axis, count, mine, act):
        @pl.loop(1, count)
        def _(step):
            act({axis: lax.rem(mine + step, count)}, lax.rem(mine + step, count))

    barrier = pltpu.get_barrier_semaphore()

    def greet(device, _):
        pl.semaphore_signal(barrier, inc=1, device_id=device, device_id_type=MESH)

    each("region", REGIONS, me, greet)
    each("slot", SLOTS, slot, greet)

    def foot_copy(chunk):
        at = pl.ds(chunk * CHUNK_LANES, CHUNK_LANES)
        return pltpu.make_async_copy(foot.at[:, :, at], foot_in.at[:, :, at], foot_sem.at[chunk])

    for chunk in range(CHUNKS):
        foot_copy(chunk).start()

    def send(axis, exchange, source, target):
        count, mine = (REGIONS, me) if axis == "region" else (SLOTS, slot)

        def act(device, other):
            pltpu.make_async_remote_copy(
                src_ref=source(other),
                dst_ref=target.at[mine],
                send_sem=send_sem.at[exchange],
                recv_sem=recv_sem.at[exchange],
                device_id=device,
                device_id_type=MESH,
            ).start()

        each(axis, count, mine, act)

    def finish(axis, exchange, target):
        count, mine = (REGIONS, me) if axis == "region" else (SLOTS, slot)
        others = target.at[pl.ds(0, count - 1)]
        return pltpu.make_async_remote_copy(
            src_ref=others,
            dst_ref=others,
            send_sem=send_sem.at[exchange],
            recv_sem=recv_sem.at[exchange],
            device_id={axis: lax.rem(mine + 1, count)},
            device_id_type=MESH,
        )

    index = jnp.concatenate(
        [obs_blocks[...], jnp.zeros((REGIONS, LANES - MOST), jnp.int32)], axis=1
    )
    index_out[...] = index.reshape(REGIONS, 1, LANES)
    index_in[me] = index_out[me]
    pl.semaphore_wait(barrier, REGIONS + SLOTS - 2)
    send("region", INDEX, lambda p: index_out.at[p], index_in)

    lane = iota((REGIONS, BLOCKS), 1)
    of_region = lane_region(lane) == iota((REGIONS, BLOCKS), 0)
    by_place = (lane_place(iota((MOST, BLOCKS), 1)) == iota((MOST, BLOCKS), 0)).astype(F32)
    cell_index = jnp.dot(
        cell_blocks[...].astype(F32), by_place, precision=lax.Precision.HIGHEST,
        preferred_element_type=F32,
    )
    cell_index = jnp.sum(jnp.where(of_region, cell_index, 0.0), axis=0, keepdims=True)
    live = jnp.dot(
        counts[...].astype(F32), of_region.astype(F32), precision=lax.Precision.HIGHEST,
        preferred_element_type=F32,
    )
    live = lane_place(iota((1, BLOCKS), 1)).astype(F32) < live - 0.5
    cell_index = jnp.where(live, cell_index, -1.0)
    row = iota((CBLK, BLOCKS), 0)
    block = ((row % 256) * 2 + row // 256).astype(F32)
    onehot_c[...] = jnp.where(block == cell_index, 1.0, 0.0).astype(BF16)

    start = load_cells(flux)
    start_picked = pick(start, onehot_c[...], AS_IS)
    picked[...] = start_picked
    gap = start - load_cells(prior)
    prec = load_cells(precision)

    for chunk in range(CHUNKS):
        foot_copy(chunk).wait()

        @pl.loop(0, CHUNK_LANES // LANES)
        def _(step):
            column = chunk * (CHUNK_LANES // LANES) + step
            at = pl.ds(pl.multiple_of(column * LANES, LANES), LANES)
            for half in range(2):
                x = foot_in[:, half * 4 : half * 4 + 4, at].reshape(LANES, LANES).T
                foot_t[pl.ds(column * 2, 2), :, half * LANES : (half + 1) * LANES] = x.reshape(
                    2, BLOCK, LANES
                )

    finish("region", INDEX, index_in).wait_recv()
    arrived = index_in[...].reshape(REGIONS, LANES).astype(F32)
    row = iota((BLOCKS, REGIONS), 0)
    by_region = (lane_region(row) == iota((BLOCKS, REGIONS), 1)).astype(F32)
    target = jnp.dot(
        by_region, arrived, precision=lax.Precision.HIGHEST, preferred_element_type=F32
    )
    row = iota((BLOCKS, LANES), 0)
    target = jnp.where(lane_place(row) == iota((BLOCKS, LANES), 1), target, 0.0)
    target = jnp.sum(target, axis=1, keepdims=True)
    column = iota((BLOCKS, 256), 1)
    block = ((column % LANES) * 2 + column // LANES).astype(F32)
    onehot_a[...] = jnp.where(block == target, 1.0, 0.0).astype(BF16)

    def forward(step, fwd, reduce):
        @pl.loop(0, BLOCK // 8)
        def _(group):
            field = picked[...]
            rows = [
                jnp.sum(foot_t[group * 8 + i] * field, axis=0, keepdims=True) for i in range(8)
            ]
            part[pl.ds(pl.multiple_of(group * 8, 8), 8), :] = jnp.concatenate(rows, axis=0)

        fwd_out[step] = to_rows(part[...]).reshape(REGIONS, 4, LANES)
        fwd_in[step, me] = fwd_out[step, me]
        send("region", fwd, lambda p: fwd_out.at[step, p], fwd_in.at[step])
        finish("region", fwd, fwd_in.at[step]).wait_recv()
        came = from_rows(fwd_in[step].reshape(LANES, LANES))
        dense[step] = to_rows(pick(came, onehot_a[...], AS_IS)).reshape(SLOTS, 16, LANES)
        sums[step, slot] = dense[step, slot]
        send("slot", reduce, lambda s: dense.at[step, s], sums.at[step])
        finish("slot", reduce, sums.at[step]).wait_recv()
        return jnp.sum(sums[step], axis=0)

    def to_sources(rows):
        return to_rows(pick(from_rows(rows), onehot_a[...], TURNED)).reshape(REGIONS, 4, LANES)

    def adjoint(came):
        part[...] = from_rows(came)

        def step(group, acc):
            for i in range(8):
                o = group * 8 + i
                acc = acc + foot_t[o] * part[pl.ds(o, 1), :]
            return acc

        term = lax.fori_loop(0, BLOCK // 8, step, jnp.zeros((BLOCK, BLOCKS), F32))
        return pick(term, onehot_c[...], TURNED)

    mine = pl.ds(pl.multiple_of(slot * 16, 16), 16)
    left = iota((1, LANES), 1) < LANES // 2

    weighted = weight[mine, :] * (forward(0, FWD0, SUM0) - value[mine, :])
    spread_out[...] = weighted
    spread[slot] = weighted
    send("slot", GATHER0, lambda s: spread_out, spread)
    finish("slot", GATHER0, spread).wait_recv()
    back_out[...] = to_sources(spread[...].reshape(LANES, LANES))
    back_in[me] = back_out[me]
    send("region", BACK0, lambda p: back_out.at[p], back_in)
    finish("region", BACK0, back_in).wait_recv()
    first = adjoint(back_in[...].reshape(LANES, LANES)) + prec * gap
    cells[...] = first

    picked[...] = pick(first, onehot_c[...], AS_IS)
    numer, denom = total(first * first), total(prec * first * first)
    image = forward(1, FWD1, SUM1)
    weighted = weight[mine, :] * image
    scalars = jnp.where(left, numer, denom + total(weighted * image))
    last_spread_out[...] = jnp.concatenate(
        [weighted, scalars, jnp.zeros((7, LANES), F32)], axis=0
    )
    last_spread[slot] = last_spread_out[...]
    send("slot", GATHER1, lambda s: last_spread_out, last_spread)
    finish("slot", GATHER1, last_spread).wait_recv()
    last_back_out[:, :4, :] = to_sources(last_spread[:, :16, :].reshape(LANES, LANES))
    scalars = jnp.sum(last_spread[:, 16, :], axis=0, keepdims=True)
    last_back_out[:, 4:5, :] = jnp.broadcast_to(scalars.reshape(1, 1, LANES), (REGIONS, 1, LANES))
    last_back_in[me] = last_back_out[me]
    send("region", BACK1, lambda p: last_back_out.at[p], last_back_in)
    finish("region", BACK1, last_back_in).wait_recv()
    scalars = jnp.sum(last_back_in[:, 4, :], axis=0, keepdims=True)
    alpha = scalars[:, 0:1] / scalars[:, LANES // 2 : LANES // 2 + 1]
    first = cells[...]
    product = adjoint(last_back_in[:, :4, :].reshape(LANES, LANES)) + prec * first

    second = first - alpha * product
    picked[...] = pick(second, onehot_c[...], AS_IS)
    gradient[...] = store_cells(second)
    increment[...] = store_cells(alpha * first)
    numer, denom = total(second * second), total(prec * second * second)
    image = forward(2, FWD2, SUM2)
    denom = denom + total(weight[mine, :] * image * image)
    slot_out[...] = jnp.where(left, numer, denom)
    slot_in[slot] = slot_out[...]
    send("slot", LAST_SLOT, lambda s: slot_out, slot_in)
    finish("slot", LAST_SLOT, slot_in).wait_recv()
    region_out[...] = jnp.sum(slot_in[...], axis=0)
    region_in[me] = region_out[...]
    send("region", LAST_REGION, lambda p: region_out, region_in)
    finish("region", LAST_REGION, region_in).wait_recv()
    scalars = jnp.sum(region_in[...], axis=0)
    alpha = scalars[:, 0:1] / scalars[:, LANES // 2 : LANES // 2 + 1]
    increment[...] = -(increment[...] + alpha * gradient[...])

    for exchange, target in (
        (INDEX, index_in), (FWD0, fwd_in.at[0]), (BACK0, back_in), (FWD1, fwd_in.at[1]),
        (BACK1, last_back_in), (FWD2, fwd_in.at[2]), (LAST_REGION, region_in),
    ):
        finish("region", exchange, target).wait_send()
    for exchange, target in (
        (SUM0, sums.at[0]), (SUM1, sums.at[1]), (SUM2, sums.at[2]), (GATHER0, spread),
        (GATHER1, last_spread), (LAST_SLOT, slot_in),
    ):
        finish("slot", exchange, target).wait_send()


def body(
    flux, prior_flux, prior_precision, obs_value, obs_weight, footprint, counts, obs_blocks,
    cell_blocks,
):
    vmem = pl.BlockSpec(memory_space=pltpu.VMEM)
    cells = (256, LANES)
    increment, gradient = pl.pallas_call(
        kernel,
        out_shape=[jax.ShapeDtypeStruct(cells, F32)] * 2,
        in_specs=[vmem] * 5 + [pl.BlockSpec(memory_space=pl.ANY)] + [vmem] * 3,
        out_specs=[vmem] * 2,
        scratch_shapes=[
            pltpu.VMEM((REGIONS, MOST, BLOCK * BLOCK), F32),
            pltpu.VMEM((BLOCK, BLOCK, BLOCKS), F32),
            pltpu.VMEM((BLOCK, BLOCKS), F32),
            pltpu.VMEM((BLOCK, BLOCKS), F32),
            pltpu.VMEM((BLOCK, CBLK), F32),
            pltpu.VMEM((CBLK, BLOCKS), BF16),
            pltpu.VMEM((BLOCKS, 256), BF16),
            pltpu.VMEM((REGIONS, 1, LANES), jnp.int32),
            pltpu.VMEM((REGIONS, 1, LANES), jnp.int32),
            pltpu.VMEM((3, REGIONS, 4, LANES), F32),
            pltpu.VMEM((3, REGIONS, 4, LANES), F32),
            pltpu.VMEM((REGIONS, 4, LANES), F32),
            pltpu.VMEM((REGIONS, 4, LANES), F32),
            pltpu.VMEM((REGIONS, 5, LANES), F32),
            pltpu.VMEM((REGIONS, 5, LANES), F32),
            pltpu.VMEM((3, SLOTS, 16, LANES), F32),
            pltpu.VMEM((3, SLOTS, 16, LANES), F32),
            pltpu.VMEM((SLOTS, 16, LANES), F32),
            pltpu.VMEM((SLOTS, 24, LANES), F32),
            pltpu.VMEM((16, LANES), F32),
            pltpu.VMEM((24, LANES), F32),
            pltpu.VMEM((1, LANES), F32),
            pltpu.VMEM((SLOTS, 1, LANES), F32),
            pltpu.VMEM((1, LANES), F32),
            pltpu.VMEM((REGIONS, 1, LANES), F32),
            pltpu.SemaphoreType.DMA((CHUNKS,)),
            pltpu.SemaphoreType.DMA((EXCHANGES,)),
            pltpu.SemaphoreType.DMA((EXCHANGES,)),
        ],
        compiler_params=pltpu.CompilerParams(
            collective_id=0, has_side_effects=True, vmem_limit_bytes=40 * 1024 * 1024
        ),
        name="inversion",
    )(
        flux.reshape(cells),
        prior_flux.reshape(cells),
        prior_precision.reshape(cells),
        obs_value.reshape(LANES, LANES),
        obs_weight.reshape(LANES, LANES),
        footprint.reshape(REGIONS, MOST, BLOCK * BLOCK),
        counts.reshape(1, REGIONS),
        obs_blocks.reshape(REGIONS, MOST),
        cell_blocks.reshape(REGIONS, MOST),
    )
    return increment.reshape(flux.shape), gradient.reshape(flux.shape)


def solution(mesh):
    placed = (
        P("slot", "region"),
        P("slot", "region"),
        P("slot", "region"),
        P("region"),
        P("region"),
        P("slot", "region", None, None, None),
        P("slot", "region", None),
        P("slot", "region", None, None),
        P("slot", "region", None, None),
    )
    return jax.shard_map(
        body,
        mesh=mesh,
        in_specs=placed,
        out_specs=(P("slot", "region"), P("slot", "region")),
        check_vma=False,
    )
```

```python
import jax
import jax.numpy as jnp
from jax import lax
from jax.experimental import pallas as pl
from jax.experimental.pallas import tpu as pltpu
from jax.sharding import PartitionSpec as P

REGIONS = 32
SLOTS = 8
MOST = 8
BLOCK = 64
BLOCKS = REGIONS * MOST
CBLK = 512
OBLK = 256
LANES = 128
CHIPS = 128
SHARE = 16
PAIRS = SHARE // 2
TILES = BLOCK // 2
MESH = pl.DeviceIdType.MESH
F32 = jnp.float32
BF16 = jnp.bfloat16
AS_IS = ((1,), (0,))
TURNED = ((1,), (1,))

FWD, BACK, LAST, CORE = (0, 1, 2), (3, 4), 5, (6, 7, 8)
EXCHANGES = 9


def hops(step):
    z, x, y = step
    return min(z, 8 - z) + min(x, 4 - x) + min(y, 4 - y)


STEPS = sorted(
    [(z, x, y) for z in range(8) for x in range(4) for y in range(4) if z or x or y],
    key=lambda step: (-hops(step), step),
)


def iota(shape, axis):
    return lax.broadcasted_iota(jnp.int32, shape, axis)


def pick(x, onehot, dims):
    high = x.astype(BF16)
    rest = x - high.astype(F32)
    middle = rest.astype(BF16)
    low = (rest - middle.astype(F32)).astype(BF16)
    pieces = jnp.concatenate([high, middle, low], axis=0)
    out = lax.dot_general(pieces, onehot, (dims, ((), ())), preferred_element_type=F32)
    rows = x.shape[0]
    return out[:rows] + out[rows : 2 * rows] + out[2 * rows :]


def load_cells(ref):
    x = ref[...]
    a, b = x[:LANES].T, x[LANES:].T
    return jnp.concatenate([a[:BLOCK], b[:BLOCK], a[BLOCK:], b[BLOCK:]], axis=1)


def store_cells(x):
    a = jnp.concatenate([x[:, :LANES], x[:, 2 * LANES : 3 * LANES]], axis=0).T
    b = jnp.concatenate([x[:, LANES : 2 * LANES], x[:, 3 * LANES :]], axis=0).T
    return jnp.concatenate([a, b], axis=0)


def total(x):
    return jnp.sum(jnp.sum(x, axis=0, keepdims=True), axis=1, keepdims=True)


def side_by_side(x):
    return jnp.concatenate([x[SHARE * k : SHARE * (k + 1)] for k in range(MOST)], axis=1)


def stacked(x):
    return jnp.concatenate([x[:, LANES * k : LANES * (k + 1)] for k in range(MOST)], axis=0)


def kernel(
    flux_hbm, prior_hbm, precision_hbm, value_hbm, weight_hbm, foot, counts_hbm, obs_hbm, cell_hbm,
    first_out, product_out, alphas,
    flux, prior, precision, value, weight, counts, obs_blocks, cell_blocks,
    foot_in, foot_t, picked, part, cells, prec, gap, onehot_c, onehot_a, observed,
    first_fwd_out, first_fwd_in, fwd_out, fwd_in, back_out, back_in, last_back_out, last_back_in,
    core_out, core_in, last_out, last_in,
    foot_sem, in_sem, send_sem, recv_sem,
):
    region, slot = lax.axis_index("region"), lax.axis_index("slot")
    y, core = lax.div(slot, 2), lax.rem(slot, 2)
    z, x = lax.div(region, 4), lax.rem(region, 4)
    me = y * REGIONS + region
    partner = {"slot": slot + 1 - 2 * core}
    at_z = [lax.rem(z + step, 8) * 4 for step in range(8)]
    at_x = [lax.rem(x + step, 4) for step in range(4)]
    at_y = [lax.rem(y + step, 4) for step in range(4)]
    slot_at = [at * 2 + core for at in at_y]
    row_at = [at * REGIONS for at in at_y]

    loads = [
        pltpu.make_async_copy(source, target, in_sem.at[i])
        for i, (source, target) in enumerate((
            (obs_hbm, obs_blocks), (cell_hbm, cell_blocks), (counts_hbm, counts), (flux_hbm, flux),
            (prior_hbm, prior), (precision_hbm, precision), (value_hbm, value), (weight_hbm, weight),
        ))
    ]

    def foot_copy(tile):
        return pltpu.make_async_copy(
            foot.at[:, pl.ds(tile * LANES, LANES)],
            foot_in.at[pl.ds(tile * BLOCKS, BLOCKS), :],
            foot_sem.at[tile],
        )

    starts = loads[:4] + [
        foot_copy(share * PAIRS + pair) for pair in range(PAIRS) for share in range(4)
    ] + loads[4:]
    barrier = pltpu.get_barrier_semaphore()
    for i, (dz, dx, dy) in enumerate(STEPS):
        pl.semaphore_signal(
            barrier, inc=1, device_id={"region": at_z[dz] + at_x[dx], "slot": slot_at[dy]},
            device_id_type=MESH,
        )
        if i % 2 == 1 and starts:
            starts.pop(0).start()
    pl.semaphore_signal(barrier, inc=1, device_id=partner, device_id_type=MESH)

    def remote(source, target, exchange, device):
        return pltpu.make_async_remote_copy(
            src_ref=source,
            dst_ref=target,
            send_sem=send_sem.at[exchange],
            recv_sem=recv_sem.at[exchange],
            device_id=device,
            device_id_type=MESH,
        )

    def send(exchange, source, target):
        for dz, dx, dy in STEPS:
            there = at_z[dz] + at_x[dx]
            remote(
                source(row_at[dy] + there), target.at[me], exchange,
                {"region": there, "slot": slot_at[dy]},
            ).start()

    def finish(exchange, target):
        others = target.at[pl.ds(0, CHIPS - 1)]
        return remote(others, others, exchange, partner)

    lane = iota((REGIONS, BLOCKS), 1)
    of_region = lane % REGIONS == iota((REGIONS, BLOCKS), 0)
    of_place = iota((MOST, BLOCKS), 1) // REGIONS == iota((MOST, BLOCKS), 0)
    loads[1].wait()
    loads[2].wait()
    cell_index = jnp.dot(
        cell_blocks[...].astype(F32), of_region.astype(F32), precision=lax.Precision.HIGHEST,
        preferred_element_type=F32,
    )
    cell_index = jnp.sum(jnp.where(of_place, cell_index, 0.0), axis=0, keepdims=True)
    live = jnp.dot(
        counts[...].astype(F32), of_region.astype(F32), precision=lax.Precision.HIGHEST,
        preferred_element_type=F32,
    )
    live = (iota((1, BLOCKS), 1) // REGIONS).astype(F32) < live - 0.5
    cell_index = jnp.where(live, cell_index, -1.0)
    row = iota((CBLK, BLOCKS), 0)
    block = ((row % 256) * 2 + row // 256).astype(F32)
    onehot_c[...] = jnp.where(block == cell_index, 1.0, 0.0).astype(BF16)

    group = iota((1, LANES), 1) // REGIONS

    def pick_cells(field):
        found = pick(field, onehot_c[...], AS_IS)
        for k in range(MOST):
            half = found[:, k // 4 * LANES : (k // 4 + 1) * LANES]
            half = jnp.where(group == k % 4, half, 0.0)
            half = half + pltpu.roll(half, 2 * REGIONS, 1)
            picked[k] = half + pltpu.roll(half, REGIONS, 1)

    loads[3].wait()
    pick_cells(load_cells(flux))

    loads[0].wait()
    index = jnp.concatenate(
        [obs_blocks[...].astype(F32), jnp.zeros((MOST, LANES - REGIONS), F32)], axis=1
    )
    index = jnp.concatenate([index, jnp.zeros((LANES - MOST, LANES), F32)], axis=0).T
    index = jnp.concatenate([index[:REGIONS]] * 4, axis=0)
    first_fwd_out[:, 1:, :] = index.reshape(CHIPS, 1, LANES)

    for pair in range(PAIRS):
        for share in range(4):
            foot_copy(share * PAIRS + pair).wait()

        @pl.loop(0, MOST)
        def _(k):
            block = [
                foot_in[pl.ds((share * PAIRS + pair) * BLOCKS + k, REGIONS, stride=MOST), :]
                for share in range(4)
            ]
            block = jnp.concatenate(block, axis=0).T
            foot_t[pl.ds(k * SHARE + 2 * pair, 2)] = block.reshape(2, BLOCK, LANES)

    def partials():
        @pl.loop(0, MOST)
        def _(k):
            field = picked[k]
            rows = [
                jnp.sum(foot_t[k * SHARE + i] * field, axis=0, keepdims=True) for i in range(SHARE)
            ]
            part[pl.ds(pl.multiple_of(k * SHARE, SHARE), SHARE), :] = jnp.concatenate(rows, axis=0)

        return part[...].T.reshape(CHIPS, 1, LANES)

    def summed(came, step, numer, denom):
        dense = pick(side_by_side(came.T), onehot_a[...], AS_IS)
        scalars = jnp.where(iota((8, OBLK), 1) < LANES, numer, denom)
        core_out[step] = jnp.concatenate([dense, scalars], axis=0)
        copy = remote(core_out.at[step], core_in.at[step], CORE[step], partner)
        copy.start()
        copy.wait_recv()
        both = core_out[step] + core_in[step]
        scalars = both[SHARE : SHARE + 1]
        return both[:SHARE], scalars[:, :1], scalars[:, LANES : LANES + 1]

    def to_sources(weighted):
        return stacked(pick(weighted, onehot_a[...], TURNED)).T.reshape(CHIPS, 1, LANES)

    def adjoint(came):
        part[...] = came.T
        halves = []
        for half in range(2):
            merged = jnp.zeros((BLOCK, LANES), F32)
            for place in range(4):
                k = half * 4 + place
                acc = foot_t[k * SHARE] * part[k * SHARE : k * SHARE + 1, :]
                for i in range(1, SHARE):
                    at = k * SHARE + i
                    acc = acc + foot_t[at] * part[at : at + 1, :]
                acc = acc + pltpu.roll(acc, 2 * REGIONS, 1)
                acc = acc + pltpu.roll(acc, REGIONS, 1)
                merged = jnp.where(group == place, acc, merged)
            halves.append(merged)
        return pick(jnp.concatenate(halves, axis=1), onehot_c[...], TURNED)

    left = iota((1, LANES), 1) < LANES // 2

    def ratio(rows):
        scalars = jnp.sum(rows, axis=0, keepdims=True)
        return scalars[:, :1] / scalars[:, LANES // 2 : LANES // 2 + 1]

    first_fwd_out[:, :1, :] = partials()
    first_fwd_in[me] = first_fwd_out[me]
    pl.semaphore_wait(barrier, CHIPS)
    send(FWD[0], lambda chip: first_fwd_out.at[chip], first_fwd_in)
    for load in loads[4:]:
        load.wait()
    gap[...] = load_cells(flux) - load_cells(prior)
    prec[...] = load_cells(precision)
    observed[0] = value[...].T.reshape(2, BLOCK, LANES)
    observed[1] = weight[...].T.reshape(2, BLOCK, LANES)
    mine = pl.ds(pl.multiple_of(y * SHARE, SHARE), SHARE)
    seen = jnp.concatenate([observed[0, 0, mine, :], observed[0, 1, mine, :]], axis=1)
    weights = jnp.concatenate([observed[1, 0, mine, :], observed[1, 1, mine, :]], axis=1)
    finish(FWD[0], first_fwd_in).wait_recv()
    index = first_fwd_in[:, 1, :]
    column = iota((LANES, OBLK), 1)
    block = ((column % LANES) * 2 + column // LANES).astype(F32)
    for k in range(MOST):
        onehot_a[k * LANES : (k + 1) * LANES, :] = jnp.where(
            index[:, k : k + 1] == block, 1.0, 0.0
        ).astype(BF16)
    image, _, _ = summed(first_fwd_in[:, 0, :], 0, 0.0, 0.0)
    back_out[...] = to_sources(weights * (image - seen))
    back_in[me] = back_out[me]
    send(BACK[0], lambda chip: back_out.at[chip], back_in)
    finish(BACK[0], back_in).wait_recv()
    first = adjoint(back_in[...].reshape(CHIPS, LANES)) + prec[...] * gap[...]
    cells[...] = first

    pick_cells(first)
    fwd_out[0] = partials()
    fwd_in[0, me] = fwd_out[0, me]
    send(FWD[1], lambda chip: fwd_out.at[0, chip], fwd_in.at[0])
    first = cells[...]
    first_out[...] = store_cells(first)
    square = first * first
    numer, denom = total(square), total(prec[...] * square)
    finish(FWD[1], fwd_in.at[0]).wait_recv()
    image, numer, denom = summed(fwd_in[0].reshape(CHIPS, LANES), 1, numer, denom)
    weighted = weights * image
    last_back_out[:, :1, :] = to_sources(weighted)
    scalars = jnp.where(left, numer, denom + total(weighted * image))
    last_back_out[:, 1:, :] = jnp.broadcast_to(scalars.reshape(1, 1, LANES), (CHIPS, 1, LANES))
    last_back_in[me] = last_back_out[me]
    send(BACK[1], lambda chip: last_back_out.at[chip], last_back_in)
    finish(BACK[1], last_back_in).wait_recv()
    first = cells[...]
    product = adjoint(last_back_in[:, 0, :]) + prec[...] * first
    alpha = ratio(last_back_in[:, 1, :])

    second = first - alpha * product
    cells[...] = second
    pick_cells(second)
    fwd_out[1] = partials()
    fwd_in[1, me] = fwd_out[1, me]
    send(FWD[2], lambda chip: fwd_out.at[1, chip], fwd_in.at[1])
    product_out[...] = store_cells(product)
    second = cells[...]
    square = second * second
    numer, denom = total(square), total(prec[...] * square)
    finish(FWD[2], fwd_in.at[1]).wait_recv()
    image, numer, denom = summed(fwd_in[1].reshape(CHIPS, LANES), 2, numer, denom)
    last_out[...] = jnp.where(left, numer, denom + total(weights * image * image))
    last_in[me] = last_out[...]
    send(LAST, lambda chip: last_out, last_in)
    finish(LAST, last_in).wait_recv()
    alphas[...] = jnp.where(left, alpha, ratio(last_in[...].reshape(CHIPS, LANES)))

    for exchange, target in (
        (FWD[0], first_fwd_in), (BACK[0], back_in), (FWD[1], fwd_in.at[0]),
        (BACK[1], last_back_in), (FWD[2], fwd_in.at[1]), (LAST, last_in),
    ):
        finish(exchange, target).wait_send()
    for step in range(3):
        remote(core_out.at[step], core_in.at[step], CORE[step], partner).wait_send()


def body(
    flux, prior_flux, prior_precision, obs_value, obs_weight, footprint, counts, obs_blocks,
    cell_blocks,
):
    cells = (256, LANES)
    message, double = (CHIPS, 1, LANES), (CHIPS, 2, LANES)
    first, product, alphas = pl.pallas_call(
        kernel,
        out_shape=[
            jax.ShapeDtypeStruct(cells, F32),
            jax.ShapeDtypeStruct(cells, F32),
            jax.ShapeDtypeStruct((1, LANES), F32),
        ],
        in_specs=[pl.BlockSpec(memory_space=pltpu.HBM)] * 9,
        out_specs=[pl.BlockSpec(memory_space=pltpu.VMEM)] * 3,
        scratch_shapes=[
            pltpu.VMEM(cells, F32),
            pltpu.VMEM(cells, F32),
            pltpu.VMEM(cells, F32),
            pltpu.VMEM((LANES, LANES), F32),
            pltpu.VMEM((LANES, LANES), F32),
            pltpu.VMEM((1, REGIONS), jnp.int32),
            pltpu.VMEM((MOST, REGIONS), jnp.int32),
            pltpu.VMEM((MOST, REGIONS), jnp.int32),
            pltpu.VMEM((TILES * BLOCKS, LANES), F32),
            pltpu.VMEM((MOST * SHARE, BLOCK, LANES), F32),
            pltpu.VMEM((MOST, BLOCK, LANES), F32),
            pltpu.VMEM((LANES, LANES), F32),
            pltpu.VMEM((BLOCK, CBLK), F32),
            pltpu.VMEM((BLOCK, CBLK), F32),
            pltpu.VMEM((BLOCK, CBLK), F32),
            pltpu.VMEM((CBLK, BLOCKS), BF16),
            pltpu.VMEM((MOST * LANES, OBLK), BF16),
            pltpu.VMEM((2, 2, BLOCK, LANES), F32),
            pltpu.VMEM(double, F32),
            pltpu.VMEM(double, F32),
            pltpu.VMEM((2, *message), F32),
            pltpu.VMEM((2, *message), F32),
            pltpu.VMEM(message, F32),
            pltpu.VMEM(message, F32),
            pltpu.VMEM(double, F32),
            pltpu.VMEM(double, F32),
            pltpu.VMEM((3, SHARE + 8, OBLK), F32),
            pltpu.VMEM((3, SHARE + 8, OBLK), F32),
            pltpu.VMEM((1, LANES), F32),
            pltpu.VMEM(message, F32),
            pltpu.SemaphoreType.DMA((TILES,)),
            pltpu.SemaphoreType.DMA((8,)),
            pltpu.SemaphoreType.DMA((EXCHANGES,)),
            pltpu.SemaphoreType.DMA((EXCHANGES,)),
        ],
        compiler_params=pltpu.CompilerParams(
            collective_id=0, has_side_effects=True, vmem_limit_bytes=60 * 1024 * 1024
        ),
        name="inversion",
    )(
        flux.reshape(cells),
        prior_flux.reshape(cells),
        prior_precision.reshape(cells),
        obs_value.reshape(LANES, LANES),
        obs_weight.reshape(LANES, LANES),
        footprint.reshape(BLOCKS, BLOCK * BLOCK),
        counts.reshape(1, REGIONS),
        obs_blocks.reshape(REGIONS, MOST).T,
        cell_blocks.reshape(REGIONS, MOST).T,
    )
    alpha, last_alpha = alphas[0, 0], alphas[0, LANES - 1]
    gradient = first - alpha * product
    increment = -(alpha * first + last_alpha * gradient)
    return increment.reshape(flux.shape), gradient.reshape(flux.shape)


def solution(mesh):
    placed = (
        P("slot", "region"),
        P("slot", "region"),
        P("slot", "region"),
        P("region"),
        P("region"),
        P("slot", "region", None, None, None),
        P("slot", "region", None),
        P("slot", "region", None, None),
        P("slot", "region", None, None),
    )
    return jax.shard_map(
        body,
        mesh=mesh,
        in_specs=placed,
        out_specs=(P("slot", "region"), P("slot", "region")),
        check_vma=False,
    )
```

```python
import jax
import jax.numpy as jnp
from jax import lax
from jax.experimental import pallas as pl
from jax.experimental.pallas import tpu as pltpu
from jax.sharding import PartitionSpec as P

REGIONS = 32
SLOTS = 8
MOST = 8
BLOCK = 64
BLOCKS = REGIONS * MOST
CBLK = 512
OBLK = 256
LANES = 128
CHIPS = 128
SHARE = 16
PAIRS = SHARE // 2
TILES = BLOCK // 2
MESH = pl.DeviceIdType.MESH
F32 = jnp.float32
BF16 = jnp.bfloat16
AS_IS = ((1,), (0,))
TURNED = ((1,), (1,))

FWD, BACK, LAST, CORE = (0, 1, 2), (3, 4), 5, (6, 7, 8)
EXCHANGES = 9


def hops(step):
    z, x, y = step
    return min(z, 8 - z) + min(x, 4 - x) + min(y, 4 - y)


STEPS = sorted(
    [(z, x, y) for z in range(8) for x in range(4) for y in range(4) if z or x or y],
    key=lambda step: (-hops(step), step),
)


def iota(shape, axis):
    return lax.broadcasted_iota(jnp.int32, shape, axis)


def pick(x, onehot, dims):
    high = x.astype(BF16)
    rest = x - high.astype(F32)
    middle = rest.astype(BF16)
    low = (rest - middle.astype(F32)).astype(BF16)
    pieces = jnp.concatenate([high, middle, low], axis=0)
    out = lax.dot_general(pieces, onehot, (dims, ((), ())), preferred_element_type=F32)
    rows = x.shape[0]
    return out[:rows] + out[rows : 2 * rows] + out[2 * rows :]


def load_cells(ref):
    x = ref[...]
    a, b = x[:LANES].T, x[LANES:].T
    return jnp.concatenate([a[:BLOCK], b[:BLOCK], a[BLOCK:], b[BLOCK:]], axis=1)


def store_cells(x):
    a = jnp.concatenate([x[:, :LANES], x[:, 2 * LANES : 3 * LANES]], axis=0).T
    b = jnp.concatenate([x[:, LANES : 2 * LANES], x[:, 3 * LANES :]], axis=0).T
    return jnp.concatenate([a, b], axis=0)


def total(x):
    return jnp.sum(jnp.sum(x, axis=0, keepdims=True), axis=1, keepdims=True)


def side_by_side(x):
    return jnp.concatenate([x[SHARE * k : SHARE * (k + 1)] for k in range(MOST)], axis=1)


def stacked(x):
    return jnp.concatenate([x[:, LANES * k : LANES * (k + 1)] for k in range(MOST)], axis=0)


def kernel(
    flux_hbm, prior_hbm, precision_hbm, value_hbm, weight_hbm, foot, counts_hbm, obs_hbm, cell_hbm,
    increment, gradient_hbm,
    flux, prior, precision, value, weight, counts, obs_blocks, cell_blocks,
    foot_in, foot_t, picked, part, cells, prec, gap, onehot_c, onehot_a, observed,
    first_fwd_out, first_fwd_in, fwd_out, fwd_in, back_out, back_in, last_back_out, last_back_in,
    core_out, core_in, last_out, last_in, gradient,
    foot_sem, in_sem, send_sem, recv_sem, out_sem,
):
    region, slot = lax.axis_index("region"), lax.axis_index("slot")
    y, core = lax.div(slot, 2), lax.rem(slot, 2)
    z, x = lax.div(region, 4), lax.rem(region, 4)
    me = y * REGIONS + region
    partner = {"slot": slot + 1 - 2 * core}
    at_z = [lax.rem(z + step, 8) * 4 for step in range(8)]
    at_x = [lax.rem(x + step, 4) for step in range(4)]
    at_y = [lax.rem(y + step, 4) for step in range(4)]
    slot_at = [at * 2 + core for at in at_y]
    row_at = [at * REGIONS for at in at_y]

    loads = [
        pltpu.make_async_copy(source, target, in_sem.at[i])
        for i, (source, target) in enumerate((
            (obs_hbm, obs_blocks), (cell_hbm, cell_blocks), (counts_hbm, counts), (flux_hbm, flux),
            (prior_hbm, prior), (precision_hbm, precision), (value_hbm, value), (weight_hbm, weight),
        ))
    ]

    def foot_copy(tile):
        return pltpu.make_async_copy(
            foot.at[:, pl.ds(tile * LANES, LANES)],
            foot_in.at[pl.ds(tile * BLOCKS, BLOCKS), :],
            foot_sem.at[tile],
        )

    starts = loads[:4] + [
        foot_copy(share * PAIRS + pair) for pair in range(PAIRS) for share in range(4)
    ] + loads[4:]
    barrier = pltpu.get_barrier_semaphore()
    for i, (dz, dx, dy) in enumerate(STEPS):
        pl.semaphore_signal(
            barrier, inc=1, device_id={"region": at_z[dz] + at_x[dx], "slot": slot_at[dy]},
            device_id_type=MESH,
        )
        if i % 2 == 1 and starts:
            starts.pop(0).start()
    pl.semaphore_signal(barrier, inc=1, device_id=partner, device_id_type=MESH)

    def remote(source, target, exchange, device):
        return pltpu.make_async_remote_copy(
            src_ref=source,
            dst_ref=target,
            send_sem=send_sem.at[exchange],
            recv_sem=recv_sem.at[exchange],
            device_id=device,
            device_id_type=MESH,
        )

    def send(exchange, source, target):
        for dz, dx, dy in STEPS:
            there = at_z[dz] + at_x[dx]
            remote(
                source(row_at[dy] + there), target.at[me], exchange,
                {"region": there, "slot": slot_at[dy]},
            ).start()

    def finish(exchange, target):
        others = target.at[pl.ds(0, CHIPS - 1)]
        return remote(others, others, exchange, partner)

    lane = iota((REGIONS, BLOCKS), 1)
    of_region = lane % REGIONS == iota((REGIONS, BLOCKS), 0)
    of_place = iota((MOST, BLOCKS), 1) // REGIONS == iota((MOST, BLOCKS), 0)
    loads[1].wait()
    loads[2].wait()
    cell_index = jnp.dot(
        cell_blocks[...].astype(F32), of_region.astype(F32), precision=lax.Precision.HIGHEST,
        preferred_element_type=F32,
    )
    cell_index = jnp.sum(jnp.where(of_place, cell_index, 0.0), axis=0, keepdims=True)
    live = jnp.dot(
        counts[...].astype(F32), of_region.astype(F32), precision=lax.Precision.HIGHEST,
        preferred_element_type=F32,
    )
    live = (iota((1, BLOCKS), 1) // REGIONS).astype(F32) < live - 0.5
    cell_index = jnp.where(live, cell_index, -1.0)
    row = iota((CBLK, BLOCKS), 0)
    block = ((row % 256) * 2 + row // 256).astype(F32)
    onehot_c[...] = jnp.where(block == cell_index, 1.0, 0.0).astype(BF16)

    group = iota((1, LANES), 1) // REGIONS

    def pick_cells(field):
        found = pick(field, onehot_c[...], AS_IS)
        for k in range(MOST):
            half = found[:, k // 4 * LANES : (k // 4 + 1) * LANES]
            half = jnp.where(group == k % 4, half, 0.0)
            half = half + pltpu.roll(half, 2 * REGIONS, 1)
            picked[k] = half + pltpu.roll(half, REGIONS, 1)

    loads[3].wait()
    pick_cells(load_cells(flux))

    loads[0].wait()
    index = jnp.concatenate(
        [obs_blocks[...].astype(F32), jnp.zeros((MOST, LANES - REGIONS), F32)], axis=1
    )
    index = jnp.concatenate([index, jnp.zeros((LANES - MOST, LANES), F32)], axis=0).T
    index = jnp.concatenate([index[:REGIONS]] * 4, axis=0)
    first_fwd_out[:, 1:, :] = index.reshape(CHIPS, 1, LANES)

    for pair in range(PAIRS):
        for share in range(4):
            foot_copy(share * PAIRS + pair).wait()

        @pl.loop(0, MOST, unroll=MOST)
        def _(k):
            block = [
                foot_in[pl.ds((share * PAIRS + pair) * BLOCKS + k, REGIONS, stride=MOST), :]
                for share in range(4)
            ]
            block = jnp.concatenate(block, axis=0).T
            foot_t[pl.ds(k * SHARE + 2 * pair, 2)] = block.reshape(2, BLOCK, LANES)

    def partials():
        @pl.loop(0, MOST)
        def _(k):
            field = picked[k]
            rows = [
                jnp.sum(foot_t[k * SHARE + i] * field, axis=0, keepdims=True) for i in range(SHARE)
            ]
            part[pl.ds(pl.multiple_of(k * SHARE, SHARE), SHARE), :] = jnp.concatenate(rows, axis=0)

        return part[...].T.reshape(CHIPS, 1, LANES)

    def summed(came, step, numer, denom):
        dense = pick(side_by_side(came.T), onehot_a[...], AS_IS)
        scalars = jnp.where(iota((8, OBLK), 1) < LANES, numer, denom)
        core_out[step] = jnp.concatenate([dense, scalars], axis=0)
        copy = remote(core_out.at[step], core_in.at[step], CORE[step], partner)
        copy.start()
        copy.wait_recv()
        both = core_out[step] + core_in[step]
        scalars = both[SHARE : SHARE + 1]
        return both[:SHARE], scalars[:, :1], scalars[:, LANES : LANES + 1]

    def to_sources(weighted):
        return stacked(pick(weighted, onehot_a[...], TURNED)).T.reshape(CHIPS, 1, LANES)

    def adjoint(came):
        part[...] = came.T
        halves = []
        for half in range(2):
            merged = jnp.zeros((BLOCK, LANES), F32)
            for place in range(4):
                k = half * 4 + place
                acc = foot_t[k * SHARE] * part[k * SHARE : k * SHARE + 1, :]
                for i in range(1, SHARE):
                    at = k * SHARE + i
                    acc = acc + foot_t[at] * part[at : at + 1, :]
                acc = acc + pltpu.roll(acc, 2 * REGIONS, 1)
                acc = acc + pltpu.roll(acc, REGIONS, 1)
                merged = jnp.where(group == place, acc, merged)
            halves.append(merged)
        return pick(jnp.concatenate(halves, axis=1), onehot_c[...], TURNED)

    left = iota((1, LANES), 1) < LANES // 2

    def ratio(rows):
        scalars = jnp.sum(rows, axis=0, keepdims=True)
        return scalars[:, :1] / scalars[:, LANES // 2 : LANES // 2 + 1]

    first_fwd_out[:, :1, :] = partials()
    first_fwd_in[me] = first_fwd_out[me]
    pl.semaphore_wait(barrier, CHIPS)
    send(FWD[0], lambda chip: first_fwd_out.at[chip], first_fwd_in)
    for load in loads[4:]:
        load.wait()
    gap[...] = load_cells(flux) - load_cells(prior)
    prec[...] = load_cells(precision)
    observed[0] = value[...].T.reshape(2, BLOCK, LANES)
    observed[1] = weight[...].T.reshape(2, BLOCK, LANES)
    mine = pl.ds(pl.multiple_of(y * SHARE, SHARE), SHARE)
    seen = jnp.concatenate([observed[0, 0, mine, :], observed[0, 1, mine, :]], axis=1)
    weights = jnp.concatenate([observed[1, 0, mine, :], observed[1, 1, mine, :]], axis=1)
    finish(FWD[0], first_fwd_in).wait_recv()
    index = first_fwd_in[:, 1, :]
    column = iota((LANES, OBLK), 1)
    block = ((column % LANES) * 2 + column // LANES).astype(F32)
    for k in range(MOST):
        onehot_a[k * LANES : (k + 1) * LANES, :] = jnp.where(
            index[:, k : k + 1] == block, 1.0, 0.0
        ).astype(BF16)
    image, _, _ = summed(first_fwd_in[:, 0, :], 0, 0.0, 0.0)
    back_out[...] = to_sources(weights * (image - seen))
    back_in[me] = back_out[me]
    send(BACK[0], lambda chip: back_out.at[chip], back_in)
    finish(BACK[0], back_in).wait_recv()
    first = adjoint(back_in[...].reshape(CHIPS, LANES)) + prec[...] * gap[...]
    cells[...] = first

    pick_cells(first)
    fwd_out[0] = partials()
    fwd_in[0, me] = fwd_out[0, me]
    send(FWD[1], lambda chip: fwd_out.at[0, chip], fwd_in.at[0])
    first = cells[...]
    increment[...] = store_cells(first)
    square = first * first
    numer, denom = total(square), total(prec[...] * square)
    finish(FWD[1], fwd_in.at[0]).wait_recv()
    image, numer, denom = summed(fwd_in[0].reshape(CHIPS, LANES), 1, numer, denom)
    weighted = weights * image
    last_back_out[:, :1, :] = to_sources(weighted)
    scalars = jnp.where(left, numer, denom + total(weighted * image))
    last_back_out[:, 1:, :] = jnp.broadcast_to(scalars.reshape(1, 1, LANES), (CHIPS, 1, LANES))
    last_back_in[me] = last_back_out[me]
    send(BACK[1], lambda chip: last_back_out.at[chip], last_back_in)
    finish(BACK[1], last_back_in).wait_recv()
    first = cells[...]
    product = adjoint(last_back_in[:, 0, :]) + prec[...] * first
    alpha = ratio(last_back_in[:, 1, :])

    second = first - alpha * product
    cells[...] = second
    pick_cells(second)
    fwd_out[1] = partials()
    fwd_in[1, me] = fwd_out[1, me]
    send(FWD[2], lambda chip: fwd_out.at[1, chip], fwd_in.at[1])
    second = cells[...]
    gradient[...] = store_cells(second)
    result = pltpu.make_async_copy(gradient, gradient_hbm, out_sem)
    result.start()
    increment[...] = increment[...] * alpha
    square = second * second
    numer, denom = total(square), total(prec[...] * square)
    finish(FWD[2], fwd_in.at[1]).wait_recv()
    image, numer, denom = summed(fwd_in[1].reshape(CHIPS, LANES), 2, numer, denom)
    last_out[...] = jnp.where(left, numer, denom + total(weights * image * image))
    last_in[me] = last_out[...]
    send(LAST, lambda chip: last_out, last_in)
    finish(LAST, last_in).wait_recv()
    alpha = ratio(last_in[...].reshape(CHIPS, LANES))
    increment[...] = -(increment[...] + alpha * gradient[...])
    result.wait()

    for exchange, target in (
        (FWD[0], first_fwd_in), (BACK[0], back_in), (FWD[1], fwd_in.at[0]),
        (BACK[1], last_back_in), (FWD[2], fwd_in.at[1]), (LAST, last_in),
    ):
        finish(exchange, target).wait_send()
    for step in range(3):
        remote(core_out.at[step], core_in.at[step], CORE[step], partner).wait_send()


def hand_over(a, b, a_out, b_out, a_held, b_held, sem):
    both = ((a, a_held, a_out, 0), (b, b_held, b_out, 1))
    for source, held, _, i in both:
        pltpu.make_async_copy(source, held, sem.at[i]).start()
    for source, held, target, i in both:
        pltpu.make_async_copy(source, held, sem.at[i]).wait()
        pltpu.make_async_copy(held, target, sem.at[i + 2]).start()
    for _, held, target, i in both:
        pltpu.make_async_copy(held, target, sem.at[i + 2]).wait()


def body(
    flux, prior_flux, prior_precision, obs_value, obs_weight, footprint, counts, obs_blocks,
    cell_blocks,
):
    cells = (256, LANES)
    message, double = (CHIPS, 1, LANES), (CHIPS, 2, LANES)
    results = pl.pallas_call(
        kernel,
        out_shape=[jax.ShapeDtypeStruct(cells, F32)] * 2,
        in_specs=[pl.BlockSpec(memory_space=pltpu.HBM)] * 9,
        out_specs=[pl.BlockSpec(memory_space=pltpu.VMEM), pl.BlockSpec(memory_space=pltpu.HBM)],
        scratch_shapes=[
            pltpu.VMEM(cells, F32),
            pltpu.VMEM(cells, F32),
            pltpu.VMEM(cells, F32),
            pltpu.VMEM((LANES, LANES), F32),
            pltpu.VMEM((LANES, LANES), F32),
            pltpu.VMEM((1, REGIONS), jnp.int32),
            pltpu.VMEM((MOST, REGIONS), jnp.int32),
            pltpu.VMEM((MOST, REGIONS), jnp.int32),
            pltpu.VMEM((TILES * BLOCKS, LANES), F32),
            pltpu.VMEM((MOST * SHARE, BLOCK, LANES), F32),
            pltpu.VMEM((MOST, BLOCK, LANES), F32),
            pltpu.VMEM((LANES, LANES), F32),
            pltpu.VMEM((BLOCK, CBLK), F32),
            pltpu.VMEM((BLOCK, CBLK), F32),
            pltpu.VMEM((BLOCK, CBLK), F32),
            pltpu.VMEM((CBLK, BLOCKS), BF16),
            pltpu.VMEM((MOST * LANES, OBLK), BF16),
            pltpu.VMEM((2, 2, BLOCK, LANES), F32),
            pltpu.VMEM(double, F32),
            pltpu.VMEM(double, F32),
            pltpu.VMEM((2, *message), F32),
            pltpu.VMEM((2, *message), F32),
            pltpu.VMEM(message, F32),
            pltpu.VMEM(message, F32),
            pltpu.VMEM(double, F32),
            pltpu.VMEM(double, F32),
            pltpu.VMEM((3, SHARE + 8, OBLK), F32),
            pltpu.VMEM((3, SHARE + 8, OBLK), F32),
            pltpu.VMEM((1, LANES), F32),
            pltpu.VMEM(message, F32),
            pltpu.VMEM(cells, F32),
            pltpu.SemaphoreType.DMA((TILES,)),
            pltpu.SemaphoreType.DMA((8,)),
            pltpu.SemaphoreType.DMA((EXCHANGES,)),
            pltpu.SemaphoreType.DMA((EXCHANGES,)),
            pltpu.SemaphoreType.DMA,
        ],
        compiler_params=pltpu.CompilerParams(
            collective_id=0, has_side_effects=True, vmem_limit_bytes=60 * 1024 * 1024
        ),
        name="inversion",
    )(
        flux.reshape(cells),
        prior_flux.reshape(cells),
        prior_precision.reshape(cells),
        obs_value.reshape(LANES, LANES),
        obs_weight.reshape(LANES, LANES),
        footprint.reshape(BLOCKS, BLOCK * BLOCK),
        counts.reshape(1, REGIONS),
        obs_blocks.reshape(REGIONS, MOST).T,
        cell_blocks.reshape(REGIONS, MOST).T,
    )
    hbm = [pl.BlockSpec(memory_space=pltpu.HBM)] * 2
    increment, gradient = pl.pallas_call(
        hand_over,
        out_shape=[jax.ShapeDtypeStruct(cells, F32)] * 2,
        in_specs=hbm,
        out_specs=hbm,
        scratch_shapes=[pltpu.VMEM(cells, F32), pltpu.VMEM(cells, F32), pltpu.SemaphoreType.DMA((4,))],
        name="hand_over",
    )(*results)
    return increment.reshape(flux.shape), gradient.reshape(flux.shape)


def solution(mesh):
    placed = (
        P("slot", "region"),
        P("slot", "region"),
        P("slot", "region"),
        P("region"),
        P("region"),
        P("slot", "region", None, None, None),
        P("slot", "region", None),
        P("slot", "region", None, None),
        P("slot", "region", None, None),
    )
    return jax.shard_map(
        body,
        mesh=mesh,
        in_specs=placed,
        out_specs=(P("slot", "region"), P("slot", "region")),
        check_vma=False,
    )
```

```python
import jax
import jax.numpy as jnp
from jax import lax
from jax.experimental import pallas as pl
from jax.experimental.pallas import tpu as pltpu
from jax.sharding import PartitionSpec as P

REGIONS = 32
SLOTS = 8
MOST = 8
BLOCK = 64
BLOCKS = REGIONS * MOST
CBLK = 512
OBLK = 256
LANES = 128
CHIPS = 128
SHARE = 16
PAIRS = SHARE // 2
TILES = BLOCK // 2
MESH = pl.DeviceIdType.MESH
F32 = jnp.float32
BF16 = jnp.bfloat16
AS_IS = ((1,), (0,))
TURNED = ((1,), (1,))

FWD, BACK, LAST, CORE = (0, 1, 2), (3, 4), 5, (6, 7, 8)
EXCHANGES = 9


def hops(step):
    z, x, y = step
    return min(z, 8 - z) + min(x, 4 - x) + min(y, 4 - y)


STEPS = sorted(
    [(z, x, y) for z in range(8) for x in range(4) for y in range(4) if z or x or y],
    key=lambda step: (-hops(step), step),
)


def iota(shape, axis):
    return lax.broadcasted_iota(jnp.int32, shape, axis)


def pick(x, onehot, dims):
    high = x.astype(BF16)
    rest = x - high.astype(F32)
    middle = rest.astype(BF16)
    low = (rest - middle.astype(F32)).astype(BF16)
    pieces = jnp.concatenate([high, middle, low], axis=0)
    out = lax.dot_general(pieces, onehot, (dims, ((), ())), preferred_element_type=F32)
    rows = x.shape[0]
    return out[:rows] + out[rows : 2 * rows] + out[2 * rows :]


def load_cells(ref):
    x = ref[...]
    a, b = x[:LANES].T, x[LANES:].T
    return jnp.concatenate([a[:BLOCK], b[:BLOCK], a[BLOCK:], b[BLOCK:]], axis=1)


def store_cells(x):
    a = jnp.concatenate([x[:, :LANES], x[:, 2 * LANES : 3 * LANES]], axis=0).T
    b = jnp.concatenate([x[:, LANES : 2 * LANES], x[:, 3 * LANES :]], axis=0).T
    return jnp.concatenate([a, b], axis=0)


def total(x):
    return jnp.sum(jnp.sum(x, axis=0, keepdims=True), axis=1, keepdims=True)


def side_by_side(x):
    return jnp.concatenate([x[SHARE * k : SHARE * (k + 1)] for k in range(MOST)], axis=1)


def stacked(x):
    return jnp.concatenate([x[:, LANES * k : LANES * (k + 1)] for k in range(MOST)], axis=0)


def kernel(
    flux_hbm, prior_hbm, precision_hbm, value_hbm, weight_hbm, foot, counts_hbm, obs_hbm, cell_hbm,
    scaled_hbm, gradient_hbm, alphas,
    flux, prior, precision, value, weight, counts, obs_blocks, cell_blocks,
    foot_in, foot_t, part, cells, prec, pull, terms, found, pulled, onehot_c, meet, onehot_a, observed,
    first_fwd_out, first_fwd_in, fwd_out, fwd_in, back_out, back_in, last_back_out, last_back_in,
    core_out, core_in, last_out, last_in, scaled, gradient,
    foot_sem, in_sem, send_sem, recv_sem, out_sem,
):
    region, slot = lax.axis_index("region"), lax.axis_index("slot")
    y, core = lax.div(slot, 2), lax.rem(slot, 2)
    z, x = lax.div(region, 4), lax.rem(region, 4)
    me = y * REGIONS + region
    partner = {"slot": slot + 1 - 2 * core}
    at_z = [lax.rem(z + step, 8) * 4 for step in range(8)]
    at_x = [lax.rem(x + step, 4) for step in range(4)]
    at_y = [lax.rem(y + step, 4) for step in range(4)]
    slot_at = [at * 2 + core for at in at_y]
    row_at = [at * REGIONS for at in at_y]

    loads = [
        pltpu.make_async_copy(source, target, in_sem.at[i])
        for i, (source, target) in enumerate((
            (obs_hbm, obs_blocks), (cell_hbm, cell_blocks), (counts_hbm, counts), (flux_hbm, flux),
            (prior_hbm, prior), (precision_hbm, precision), (value_hbm, value), (weight_hbm, weight),
        ))
    ]

    def foot_copy(tile):
        return pltpu.make_async_copy(
            foot.at[:, pl.ds(tile * LANES, LANES)],
            foot_in.at[pl.ds(tile * BLOCKS, BLOCKS), :],
            foot_sem.at[tile],
        )

    starts = loads[:4] + [
        foot_copy(share * PAIRS + pair) for pair in range(PAIRS) for share in range(4)
    ] + loads[4:]
    barrier = pltpu.get_barrier_semaphore()
    for i, (dz, dx, dy) in enumerate(STEPS):
        pl.semaphore_signal(
            barrier, inc=1, device_id={"region": at_z[dz] + at_x[dx], "slot": slot_at[dy]},
            device_id_type=MESH,
        )
        if i % 2 == 1 and starts:
            starts.pop(0).start()
    pl.semaphore_signal(barrier, inc=1, device_id=partner, device_id_type=MESH)

    def remote(source, target, exchange, device):
        return pltpu.make_async_remote_copy(
            src_ref=source,
            dst_ref=target,
            send_sem=send_sem.at[exchange],
            recv_sem=recv_sem.at[exchange],
            device_id=device,
            device_id_type=MESH,
        )

    def send(exchange, source, target, rows=1):
        for dz, dx, dy in STEPS:
            there = at_z[dz] + at_x[dx]
            chip = row_at[dy] + there if source.shape[0] > 1 else 0
            remote(
                source.at[pl.ds(chip * rows, rows), :], target.at[pl.ds(me * rows, rows), :], exchange,
                {"region": there, "slot": slot_at[dy]},
            ).start()

    def finish(exchange, target, rows=1):
        others = target.at[pl.ds(0, (CHIPS - 1) * rows), :]
        return remote(others, others, exchange, partner)

    def keep(source, target, rows=1):
        target[pl.ds(me * rows, rows), :] = source[pl.ds(me * rows, rows), :]

    def every_other(first):
        return pl.ds(first, CHIPS, stride=2)

    lane = iota((REGIONS, BLOCKS), 1)
    of_region = lane % REGIONS == iota((REGIONS, BLOCKS), 0)
    of_place = iota((MOST, BLOCKS), 1) // REGIONS == iota((MOST, BLOCKS), 0)
    loads[1].wait()
    loads[2].wait()
    cell_index = jnp.dot(
        cell_blocks[...].astype(F32), of_region.astype(F32), precision=lax.Precision.HIGHEST,
        preferred_element_type=F32,
    )
    cell_index = jnp.sum(jnp.where(of_place, cell_index, 0.0), axis=0, keepdims=True)
    live = jnp.dot(
        counts[...].astype(F32), of_region.astype(F32), precision=lax.Precision.HIGHEST,
        preferred_element_type=F32,
    )
    live = (iota((1, BLOCKS), 1) // REGIONS).astype(F32) < live - 0.5
    cell_index = jnp.where(live, cell_index, -1.0)
    row = iota((CBLK, BLOCKS), 0)
    block = ((row % 256) * 2 + row // 256).astype(F32)
    onehot_c[...] = jnp.where(block == cell_index, 1.0, 0.0).astype(BF16)

    group = iota((1, LANES), 1) // REGIONS

    loads[3].wait()
    found[...] = pick(load_cells(flux), onehot_c[...], AS_IS)

    loads[0].wait()
    index = jnp.concatenate(
        [obs_blocks[...].astype(F32), jnp.zeros((MOST, LANES - REGIONS), F32)], axis=1
    )
    index = jnp.concatenate([index, jnp.zeros((LANES - MOST, LANES), F32)], axis=0).T
    index = jnp.concatenate([index[:REGIONS]] * 4, axis=0)
    first_fwd_out[every_other(1), :] = index

    for pair in range(PAIRS):
        for share in range(4):
            foot_copy(share * PAIRS + pair).wait()

        @pl.loop(0, MOST, unroll=MOST)
        def _(k):
            block = [
                foot_in[pl.ds((share * PAIRS + pair) * BLOCKS + k, REGIONS, stride=MOST), :]
                for share in range(4)
            ]
            block = jnp.concatenate(block, axis=0).T
            foot_t[pl.ds(k * SHARE + 2 * pair, 2)] = block.reshape(2, BLOCK, LANES)

    low = [iota((8, LANES), 0) // shift % 2 == 0 for shift in (1, 2, 4)]

    def partials(picked):
        rows = []
        for k in range(MOST):
            field = picked[:, k // 4 * LANES : (k // 4 + 1) * LANES]
            field = jnp.where(group == k % 4, field, 0.0)
            field = field + pltpu.roll(field, 2 * REGIONS, 1)
            field = field + pltpu.roll(field, REGIONS, 1)
            for start in range(0, SHARE, 8):
                sums = []
                for i in range(start, start + 8):
                    acc = foot_t[k * SHARE + i, :8, :] * field[:8]
                    for c in range(8, BLOCK, 8):
                        acc = acc + foot_t[k * SHARE + i, c : c + 8, :] * field[c : c + 8]
                    sums.append(acc)
                for mask, shift in zip(low, (1, 2, 4)):
                    sums = [
                        jnp.where(mask, a, b) + pltpu.roll(jnp.where(mask, b, a), 8 - shift, 0)
                        for a, b in zip(sums[::2], sums[1::2])
                    ]
                rows += sums
        return jnp.concatenate(rows, axis=0).T

    def summed(came, step, numer, denom):
        dense = pick(side_by_side(came.T), onehot_a[...], AS_IS)
        scalars = jnp.where(iota((8, OBLK), 1) < LANES, numer, denom)
        core_out[step] = jnp.concatenate([dense, scalars], axis=0)
        copy = remote(core_out.at[step], core_in.at[step], CORE[step], partner)
        copy.start()
        copy.wait_recv()
        both = core_out[step] + core_in[step]
        scalars = both[SHARE : SHARE + 1]
        return both[:SHARE], scalars[:, :1], scalars[:, LANES : LANES + 1]

    def to_sources(weighted):
        return stacked(pick(weighted, onehot_a[...], TURNED)).T

    def adjoint(came):
        part[...] = came.T
        halves = []
        for half in range(2):
            merged = jnp.zeros((BLOCK, LANES), F32)
            for place in range(4):
                k = half * 4 + place
                acc = foot_t[k * SHARE] * part[k * SHARE : k * SHARE + 1, :]
                for i in range(1, SHARE):
                    at = k * SHARE + i
                    acc = acc + foot_t[at] * part[at : at + 1, :]
                acc = acc + pltpu.roll(acc, 2 * REGIONS, 1)
                acc = acc + pltpu.roll(acc, REGIONS, 1)
                merged = jnp.where(group == place, acc, merged)
            halves.append(merged)
        return jnp.concatenate(halves, axis=1)

    left = iota((1, LANES), 1) < LANES // 2

    def ratio(rows):
        scalars = jnp.sum(rows, axis=0, keepdims=True)
        return scalars[:, :1] / scalars[:, LANES // 2 : LANES // 2 + 1]

    first_fwd_out[every_other(0), :] = partials(found[...])
    keep(first_fwd_out, first_fwd_in, 2)
    pl.semaphore_wait(barrier, CHIPS)
    send(FWD[0], first_fwd_out, first_fwd_in, 2)
    for load in loads[4:]:
        load.wait()
    prec[...] = load_cells(precision)
    pull[...] = prec[...] * (load_cells(flux) - load_cells(prior))
    pulled[...] = pick(pull[...], onehot_c[...], AS_IS)
    meet[...] = lax.dot_general(
        onehot_c[...], onehot_c[...], (((0,), (0,)), ((), ())), preferred_element_type=F32
    ).astype(BF16)
    observed[0] = value[...].T.reshape(2, BLOCK, LANES)
    observed[1] = weight[...].T.reshape(2, BLOCK, LANES)
    mine = pl.ds(pl.multiple_of(y * SHARE, SHARE), SHARE)
    seen = jnp.concatenate([observed[0, 0, mine, :], observed[0, 1, mine, :]], axis=1)
    weights = jnp.concatenate([observed[1, 0, mine, :], observed[1, 1, mine, :]], axis=1)
    finish(FWD[0], first_fwd_in, 2).wait_recv()
    index = first_fwd_in[every_other(1), :]
    column = iota((LANES, OBLK), 1)
    block = ((column % LANES) * 2 + column // LANES).astype(F32)
    for k in range(MOST):
        onehot_a[k * LANES : (k + 1) * LANES, :] = jnp.where(
            index[:, k : k + 1] == block, 1.0, 0.0
        ).astype(BF16)
    image, _, _ = summed(first_fwd_in[every_other(0), :], 0, 0.0, 0.0)
    back_out[...] = to_sources(weights * (image - seen))
    keep(back_out, back_in)
    send(BACK[0], back_out, back_in)
    finish(BACK[0], back_in).wait_recv()

    term = adjoint(back_in[...])
    terms[...] = term
    picked = pick(term, meet[...], AS_IS) + pulled[...]
    found[...] = picked
    fwd_out[0] = partials(picked)
    keep(fwd_out.at[0], fwd_in.at[0])
    send(FWD[1], fwd_out.at[0], fwd_in.at[0])
    first = pick(terms[...], onehot_c[...], TURNED) + pull[...]
    cells[...] = first
    pulled[...] = pick(prec[...] * first, onehot_c[...], AS_IS)
    scaled[...] = store_cells(first)
    square = first * first
    numer, denom = total(square), total(prec[...] * square)
    finish(FWD[1], fwd_in.at[0]).wait_recv()
    image, numer, denom = summed(fwd_in[0], 1, numer, denom)
    weighted = weights * image
    last_back_out[every_other(0), :] = to_sources(weighted)
    scalars = jnp.where(left, numer, denom + total(weighted * image))
    last_back_out[every_other(1), :] = jnp.broadcast_to(scalars, (CHIPS, LANES))
    keep(last_back_out, last_back_in, 2)
    send(BACK[1], last_back_out, last_back_in, 2)
    finish(BACK[1], last_back_in, 2).wait_recv()
    alpha = ratio(last_back_in[every_other(1), :])

    term = adjoint(last_back_in[every_other(0), :])
    terms[...] = term
    picked = found[...] - alpha * (pick(term, meet[...], AS_IS) + pulled[...])
    fwd_out[1] = partials(picked)
    keep(fwd_out.at[1], fwd_in.at[1])
    send(FWD[2], fwd_out.at[1], fwd_in.at[1])
    first = cells[...]
    second = first - alpha * (pick(terms[...], onehot_c[...], TURNED) + prec[...] * first)
    gradient[...] = store_cells(second)
    scaled[...] = scaled[...] * alpha
    results = [
        pltpu.make_async_copy(gradient, gradient_hbm, out_sem.at[0]),
        pltpu.make_async_copy(scaled, scaled_hbm, out_sem.at[1]),
    ]
    for result in results:
        result.start()
    square = second * second
    numer, denom = total(square), total(prec[...] * square)
    finish(FWD[2], fwd_in.at[1]).wait_recv()
    image, numer, denom = summed(fwd_in[1], 2, numer, denom)
    last_out[...] = jnp.where(left, numer, denom + total(weights * image * image))
    last_in[pl.ds(me, 1), :] = last_out[...]
    send(LAST, last_out, last_in)
    finish(LAST, last_in).wait_recv()
    alphas[...] = jnp.broadcast_to(ratio(last_in[...]), (1, LANES))
    for result in results:
        result.wait()

    for exchange, target, rows in (
        (FWD[0], first_fwd_in, 2), (BACK[0], back_in, 1), (FWD[1], fwd_in.at[0], 1),
        (BACK[1], last_back_in, 2), (FWD[2], fwd_in.at[1], 1), (LAST, last_in, 1),
    ):
        finish(exchange, target, rows).wait_send()
    for step in range(3):
        remote(core_out.at[step], core_in.at[step], CORE[step], partner).wait_send()


def finish_step(scaled, gradient, alphas, increment_out, gradient_out, a, b, c, d, sem):
    copies = [
        pltpu.make_async_copy(source, target, sem.at[i])
        for i, (source, target) in enumerate(
            ((alphas, c), (gradient, b), (scaled, a), (b, gradient_out), (d, increment_out))
        )
    ]
    for copy in copies[:3]:
        copy.start()
    copies[1].wait()
    copies[3].start()
    copies[0].wait()
    copies[2].wait()
    d[...] = -(a[...] + c[...] * b[...])
    copies[4].start()
    copies[3].wait()
    copies[4].wait()


def body(
    flux, prior_flux, prior_precision, obs_value, obs_weight, footprint, counts, obs_blocks,
    cell_blocks,
):
    cells = (256, LANES)
    message, double = (CHIPS, LANES), (2 * CHIPS, LANES)
    results = pl.pallas_call(
        kernel,
        out_shape=[jax.ShapeDtypeStruct(cells, F32)] * 2 + [jax.ShapeDtypeStruct((1, LANES), F32)],
        in_specs=[pl.BlockSpec(memory_space=pltpu.HBM)] * 9,
        out_specs=[pl.BlockSpec(memory_space=pltpu.HBM)] * 2 + [pl.BlockSpec(memory_space=pltpu.VMEM)],
        scratch_shapes=[
            pltpu.VMEM(cells, F32),
            pltpu.VMEM(cells, F32),
            pltpu.VMEM(cells, F32),
            pltpu.VMEM((LANES, LANES), F32),
            pltpu.VMEM((LANES, LANES), F32),
            pltpu.VMEM((1, REGIONS), jnp.int32),
            pltpu.VMEM((MOST, REGIONS), jnp.int32),
            pltpu.VMEM((MOST, REGIONS), jnp.int32),
            pltpu.VMEM((TILES * BLOCKS, LANES), F32),
            pltpu.VMEM((MOST * SHARE, BLOCK, LANES), F32),
            pltpu.VMEM((LANES, LANES), F32),
            pltpu.VMEM((BLOCK, CBLK), F32),
            pltpu.VMEM((BLOCK, CBLK), F32),
            pltpu.VMEM((BLOCK, CBLK), F32),
            pltpu.VMEM((BLOCK, BLOCKS), F32),
            pltpu.VMEM((BLOCK, BLOCKS), F32),
            pltpu.VMEM((BLOCK, BLOCKS), F32),
            pltpu.VMEM((CBLK, BLOCKS), BF16),
            pltpu.VMEM((BLOCKS, BLOCKS), BF16),
            pltpu.VMEM((MOST * LANES, OBLK), BF16),
            pltpu.VMEM((2, 2, BLOCK, LANES), F32),
            pltpu.VMEM(double, F32),
            pltpu.VMEM(double, F32),
            pltpu.VMEM((2, *message), F32),
            pltpu.VMEM((2, *message), F32),
            pltpu.VMEM(message, F32),
            pltpu.VMEM(message, F32),
            pltpu.VMEM(double, F32),
            pltpu.VMEM(double, F32),
            pltpu.VMEM((3, SHARE + 8, OBLK), F32),
            pltpu.VMEM((3, SHARE + 8, OBLK), F32),
            pltpu.VMEM((1, LANES), F32),
            pltpu.VMEM(message, F32),
            pltpu.VMEM(cells, F32),
            pltpu.VMEM(cells, F32),
            pltpu.SemaphoreType.DMA((TILES,)),
            pltpu.SemaphoreType.DMA((8,)),
            pltpu.SemaphoreType.DMA((EXCHANGES,)),
            pltpu.SemaphoreType.DMA((EXCHANGES,)),
            pltpu.SemaphoreType.DMA((2,)),
        ],
        compiler_params=pltpu.CompilerParams(
            collective_id=0, has_side_effects=True, vmem_limit_bytes=60 * 1024 * 1024
        ),
        name="inversion",
    )(
        flux.reshape(cells),
        prior_flux.reshape(cells),
        prior_precision.reshape(cells),
        obs_value.reshape(LANES, LANES),
        obs_weight.reshape(LANES, LANES),
        footprint.reshape(BLOCKS, BLOCK * BLOCK),
        counts.reshape(1, REGIONS),
        obs_blocks.reshape(REGIONS, MOST).T,
        cell_blocks.reshape(REGIONS, MOST).T,
    )
    hbm = [pl.BlockSpec(memory_space=pltpu.HBM)]
    increment, gradient = pl.pallas_call(
        finish_step,
        out_shape=[jax.ShapeDtypeStruct(cells, F32)] * 2,
        in_specs=hbm * 3,
        out_specs=hbm * 2,
        scratch_shapes=[
            pltpu.VMEM(cells, F32),
            pltpu.VMEM(cells, F32),
            pltpu.VMEM((1, LANES), F32),
            pltpu.VMEM(cells, F32),
            pltpu.SemaphoreType.DMA((5,)),
        ],
        name="finish_step",
    )(*results)
    return increment.reshape(flux.shape), gradient.reshape(flux.shape)


def solution(mesh):
    placed = (
        P("slot", "region"),
        P("slot", "region"),
        P("slot", "region"),
        P("region"),
        P("region"),
        P("slot", "region", None, None, None),
        P("slot", "region", None),
        P("slot", "region", None, None),
        P("slot", "region", None, None),
    )
    return jax.shard_map(
        body,
        mesh=mesh,
        in_specs=placed,
        out_specs=(P("slot", "region"), P("slot", "region")),
        check_vma=False,
    )
```

```python
import jax
import jax.numpy as jnp
from jax import lax
from jax.experimental import pallas as pl
from jax.experimental.pallas import tpu as pltpu
from jax.sharding import PartitionSpec as P

REGIONS = 32
SLOTS = 8
MOST = 8
BLOCK = 64
BLOCKS = REGIONS * MOST
CBLK = 512
OBLK = 256
LANES = 128
CHIPS = 128
SHARE = 16
PAIRS = SHARE // 2
TILES = BLOCK // 2
MESH = pl.DeviceIdType.MESH
F32 = jnp.float32
BF16 = jnp.bfloat16
AS_IS = ((1,), (0,))
TURNED = ((1,), (1,))

FWD, BACK, LAST, CORE, SUMS = (0, 1, 2), (3, 4), 5, (6, 7, 8), 9
EXCHANGES = 10


def hops(step):
    z, x, y = step
    return min(z, 8 - z) + min(x, 4 - x) + min(y, 4 - y)


STEPS = sorted(
    [(z, x, y) for z in range(8) for x in range(4) for y in range(4) if z or x or y],
    key=lambda step: (-hops(step), step),
)


def iota(shape, axis):
    return lax.broadcasted_iota(jnp.int32, shape, axis)


def pick(x, onehot, dims):
    high = x.astype(BF16)
    rest = x - high.astype(F32)
    middle = rest.astype(BF16)
    low = (rest - middle.astype(F32)).astype(BF16)
    pieces = jnp.concatenate([high, middle, low], axis=0)
    out = lax.dot_general(pieces, onehot, (dims, ((), ())), preferred_element_type=F32)
    rows = x.shape[0]
    return out[:rows] + out[rows : 2 * rows] + out[2 * rows :]


def load_cells(ref):
    x = ref[...]
    a, b = x[:LANES].T, x[LANES:].T
    return jnp.concatenate([a[:BLOCK], b[:BLOCK], a[BLOCK:], b[BLOCK:]], axis=1)


def store_cells(x):
    a = jnp.concatenate([x[:, :LANES], x[:, 2 * LANES : 3 * LANES]], axis=0).T
    b = jnp.concatenate([x[:, LANES : 2 * LANES], x[:, 3 * LANES :]], axis=0).T
    return jnp.concatenate([a, b], axis=0)


def total(x):
    return jnp.sum(jnp.sum(x, axis=0, keepdims=True), axis=1, keepdims=True)


def side_by_side(x):
    return jnp.concatenate([x[SHARE * k : SHARE * (k + 1)] for k in range(MOST)], axis=1)


def stacked(x):
    return jnp.concatenate([x[:, LANES * k : LANES * (k + 1)] for k in range(MOST)], axis=0)


def kernel(
    flux_hbm, prior_hbm, precision_hbm, value_hbm, weight_hbm, foot, counts_hbm, obs_hbm, cell_hbm,
    scaled_hbm, gradient_hbm, alphas,
    flux, prior, precision, value, weight, counts, obs_blocks, cell_blocks,
    foot_in, foot_t, part, cells, prec, pull, terms, found, pulled, onehot_c, meet, onehot_a, observed,
    first_fwd_out, first_fwd_in, fwd_out, fwd_in, back_out, back_in, last_back_out, last_back_in,
    core_out, core_in, first_image, sum_out, sum_in, last_out, last_in, scaled, gradient,
    foot_sem, in_sem, send_sem, recv_sem, out_sem,
):
    region, slot = lax.axis_index("region"), lax.axis_index("slot")
    y, core = lax.div(slot, 2), lax.rem(slot, 2)
    z, x = lax.div(region, 4), lax.rem(region, 4)
    me = y * REGIONS + region
    partner = {"slot": slot + 1 - 2 * core}
    at_z = [lax.rem(z + step, 8) * 4 for step in range(8)]
    at_x = [lax.rem(x + step, 4) for step in range(4)]
    at_y = [lax.rem(y + step, 4) for step in range(4)]
    slot_at = [at * 2 + core for at in at_y]
    row_at = [at * REGIONS for at in at_y]

    loads = [
        pltpu.make_async_copy(source, target, in_sem.at[i])
        for i, (source, target) in enumerate((
            (obs_hbm, obs_blocks), (cell_hbm, cell_blocks), (counts_hbm, counts), (flux_hbm, flux),
            (prior_hbm, prior), (precision_hbm, precision), (value_hbm, value), (weight_hbm, weight),
        ))
    ]

    def foot_copy(tile):
        return pltpu.make_async_copy(
            foot.at[:, pl.ds(tile * LANES, LANES)],
            foot_in.at[pl.ds(tile * BLOCKS, BLOCKS), :],
            foot_sem.at[tile],
        )

    starts = loads[:4] + [
        foot_copy(share * PAIRS + pair) for pair in range(PAIRS) for share in range(4)
    ] + loads[4:]
    barrier = pltpu.get_barrier_semaphore()
    for i, (dz, dx, dy) in enumerate(STEPS):
        pl.semaphore_signal(
            barrier, inc=1, device_id={"region": at_z[dz] + at_x[dx], "slot": slot_at[dy]},
            device_id_type=MESH,
        )
        if i % 2 == 1 and starts:
            starts.pop(0).start()
    pl.semaphore_signal(barrier, inc=1, device_id=partner, device_id_type=MESH)

    def remote(source, target, exchange, device):
        return pltpu.make_async_remote_copy(
            src_ref=source,
            dst_ref=target,
            send_sem=send_sem.at[exchange],
            recv_sem=recv_sem.at[exchange],
            device_id=device,
            device_id_type=MESH,
        )

    def send(exchange, source, target, rows=1):
        for dz, dx, dy in STEPS:
            there = at_z[dz] + at_x[dx]
            chip = row_at[dy] + there if source.shape[0] > 1 else 0
            remote(
                source.at[pl.ds(chip * rows, rows), :], target.at[pl.ds(me * rows, rows), :], exchange,
                {"region": there, "slot": slot_at[dy]},
            ).start()

    def finish(exchange, target, rows=1):
        others = target.at[pl.ds(0, (CHIPS - 1) * rows), :]
        return remote(others, others, exchange, partner)

    def keep(source, target, rows=1):
        target[pl.ds(me * rows, rows), :] = source[pl.ds(me * rows, rows), :]

    def every_other(first):
        return pl.ds(first, CHIPS, stride=2)

    lane = iota((REGIONS, BLOCKS), 1)
    of_region = lane % REGIONS == iota((REGIONS, BLOCKS), 0)
    of_place = iota((MOST, BLOCKS), 1) // REGIONS == iota((MOST, BLOCKS), 0)
    loads[1].wait()
    loads[2].wait()
    cell_index = jnp.dot(
        cell_blocks[...].astype(F32), of_region.astype(F32), precision=lax.Precision.HIGHEST,
        preferred_element_type=F32,
    )
    cell_index = jnp.sum(jnp.where(of_place, cell_index, 0.0), axis=0, keepdims=True)
    live = jnp.dot(
        counts[...].astype(F32), of_region.astype(F32), precision=lax.Precision.HIGHEST,
        preferred_element_type=F32,
    )
    live = (iota((1, BLOCKS), 1) // REGIONS).astype(F32) < live - 0.5
    cell_index = jnp.where(live, cell_index, -1.0)
    row = iota((CBLK, BLOCKS), 0)
    block = ((row % 256) * 2 + row // 256).astype(F32)
    onehot_c[...] = jnp.where(block == cell_index, 1.0, 0.0).astype(BF16)

    group = iota((1, LANES), 1) // REGIONS

    loads[3].wait()
    found[...] = pick(load_cells(flux), onehot_c[...], AS_IS)

    loads[0].wait()
    index = jnp.concatenate(
        [obs_blocks[...].astype(F32), jnp.zeros((MOST, LANES - REGIONS), F32)], axis=1
    )
    index = jnp.concatenate([index, jnp.zeros((LANES - MOST, LANES), F32)], axis=0).T
    index = jnp.concatenate([index[:REGIONS]] * 4, axis=0)
    first_fwd_out[every_other(1), :] = index

    for pair in range(PAIRS):
        for share in range(4):
            foot_copy(share * PAIRS + pair).wait()

        @pl.loop(0, MOST, unroll=MOST)
        def _(k):
            block = [
                foot_in[pl.ds((share * PAIRS + pair) * BLOCKS + k, REGIONS, stride=MOST), :]
                for share in range(4)
            ]
            block = jnp.concatenate(block, axis=0).T
            foot_t[pl.ds(k * SHARE + 2 * pair, 2)] = block.reshape(2, BLOCK, LANES)

    low = [iota((8, LANES), 0) // shift % 2 == 0 for shift in (1, 2, 4)]

    def partials(picked):
        rows = []
        for k in range(MOST):
            field = picked[:, k // 4 * LANES : (k // 4 + 1) * LANES]
            field = jnp.where(group == k % 4, field, 0.0)
            field = field + pltpu.roll(field, 2 * REGIONS, 1)
            field = field + pltpu.roll(field, REGIONS, 1)
            for start in range(0, SHARE, 8):
                sums = []
                for i in range(start, start + 8):
                    acc = foot_t[k * SHARE + i, :8, :] * field[:8]
                    for c in range(8, BLOCK, 8):
                        acc = acc + foot_t[k * SHARE + i, c : c + 8, :] * field[c : c + 8]
                    sums.append(acc)
                for mask, shift in zip(low, (1, 2, 4)):
                    sums = [
                        jnp.where(mask, a, b) + pltpu.roll(jnp.where(mask, b, a), 8 - shift, 0)
                        for a, b in zip(sums[::2], sums[1::2])
                    ]
                rows += sums
        return jnp.concatenate(rows, axis=0).T

    def summed(came, step, numer, denom):
        dense = pick(side_by_side(came.T), onehot_a[...], AS_IS)
        scalars = jnp.where(iota((8, OBLK), 1) < LANES, numer, denom)
        core_out[step] = jnp.concatenate([dense, scalars], axis=0)
        copy = remote(core_out.at[step], core_in.at[step], CORE[step], partner)
        copy.start()
        copy.wait_recv()
        both = core_out[step] + core_in[step]
        scalars = both[SHARE : SHARE + 1]
        return both[:SHARE], scalars[:, :1], scalars[:, LANES : LANES + 1]

    def to_sources(weighted):
        return stacked(pick(weighted, onehot_a[...], TURNED)).T

    def adjoint(came):
        part[...] = came.T
        halves = []
        for half in range(2):
            merged = jnp.zeros((BLOCK, LANES), F32)
            for place in range(4):
                k = half * 4 + place
                acc = foot_t[k * SHARE] * part[k * SHARE : k * SHARE + 1, :]
                for i in range(1, SHARE):
                    at = k * SHARE + i
                    acc = acc + foot_t[at] * part[at : at + 1, :]
                acc = acc + pltpu.roll(acc, 2 * REGIONS, 1)
                acc = acc + pltpu.roll(acc, REGIONS, 1)
                merged = jnp.where(group == place, acc, merged)
            halves.append(merged)
        return jnp.concatenate(halves, axis=1)

    left = iota((1, LANES), 1) < LANES // 2

    def ratio(rows):
        scalars = jnp.sum(rows, axis=0, keepdims=True)
        return scalars[:, :1] / scalars[:, LANES // 2 : LANES // 2 + 1]

    first_fwd_out[every_other(0), :] = partials(found[...])
    keep(first_fwd_out, first_fwd_in, 2)
    pl.semaphore_wait(barrier, CHIPS)
    send(FWD[0], first_fwd_out, first_fwd_in, 2)
    for load in loads[4:]:
        load.wait()
    prec[...] = load_cells(precision)
    pull[...] = prec[...] * (load_cells(flux) - load_cells(prior))
    pulled[...] = pick(pull[...], onehot_c[...], AS_IS)
    meet[...] = lax.dot_general(
        onehot_c[...], onehot_c[...], (((0,), (0,)), ((), ())), preferred_element_type=F32
    ).astype(BF16)
    observed[0] = value[...].T.reshape(2, BLOCK, LANES)
    observed[1] = weight[...].T.reshape(2, BLOCK, LANES)
    mine = pl.ds(pl.multiple_of(y * SHARE, SHARE), SHARE)
    seen = jnp.concatenate([observed[0, 0, mine, :], observed[0, 1, mine, :]], axis=1)
    weights = jnp.concatenate([observed[1, 0, mine, :], observed[1, 1, mine, :]], axis=1)
    finish(FWD[0], first_fwd_in, 2).wait_recv()
    index = first_fwd_in[every_other(1), :]
    column = iota((LANES, OBLK), 1)
    block = ((column % LANES) * 2 + column // LANES).astype(F32)
    for k in range(MOST):
        onehot_a[k * LANES : (k + 1) * LANES, :] = jnp.where(
            index[:, k : k + 1] == block, 1.0, 0.0
        ).astype(BF16)
    image, _, _ = summed(first_fwd_in[every_other(0), :], 0, 0.0, 0.0)
    back_out[...] = to_sources(weights * (image - seen))
    keep(back_out, back_in)
    send(BACK[0], back_out, back_in)
    finish(BACK[0], back_in).wait_recv()

    term = adjoint(back_in[...])
    terms[...] = term
    picked = pick(term, meet[...], AS_IS) + pulled[...]
    fwd_out[0] = partials(picked)
    keep(fwd_out.at[0], fwd_in.at[0])
    send(FWD[1], fwd_out.at[0], fwd_in.at[0])
    first = pick(terms[...], onehot_c[...], TURNED) + pull[...]
    cells[...] = first
    pulled[...] = pick(prec[...] * first, onehot_c[...], AS_IS)
    scaled[...] = store_cells(first)
    square = first * first
    numer, denom = total(square), total(prec[...] * square)
    finish(FWD[1], fwd_in.at[0]).wait_recv()
    image, numer, denom = summed(fwd_in[0], 1, numer, denom)
    first_image[...] = image
    weighted = weights * image
    last_back_out[...] = to_sources(weighted)
    keep(last_back_out, last_back_in)
    send(BACK[1], last_back_out, last_back_in)
    sum_out[...] = jnp.where(left, numer, denom + total(weighted * image))
    sum_in[pl.ds(me, 1), :] = sum_out[...]
    send(SUMS, sum_out, sum_in)
    finish(BACK[1], last_back_in).wait_recv()

    term = adjoint(last_back_in[...])
    terms[...] = term
    picked = pick(term, meet[...], AS_IS) + pulled[...]
    fwd_out[1] = partials(picked)
    keep(fwd_out.at[1], fwd_in.at[1])
    send(FWD[2], fwd_out.at[1], fwd_in.at[1])
    finish(SUMS, sum_in).wait_recv()
    alpha = ratio(sum_in[...])
    first = cells[...]
    second = first - alpha * (pick(terms[...], onehot_c[...], TURNED) + prec[...] * first)
    gradient[...] = store_cells(second)
    scaled[...] = scaled[...] * alpha
    results = [
        pltpu.make_async_copy(gradient, gradient_hbm, out_sem.at[0]),
        pltpu.make_async_copy(scaled, scaled_hbm, out_sem.at[1]),
    ]
    for result in results:
        result.start()
    square = second * second
    numer, denom = total(square), total(prec[...] * square)
    finish(FWD[2], fwd_in.at[1]).wait_recv()
    image, numer, denom = summed(fwd_in[1], 2, numer, denom)
    image = first_image[...] - alpha * image
    last_out[...] = jnp.where(left, numer, denom + total(weights * image * image))
    last_in[pl.ds(me, 1), :] = last_out[...]
    send(LAST, last_out, last_in)
    finish(LAST, last_in).wait_recv()
    alphas[...] = jnp.broadcast_to(ratio(last_in[...]), (1, LANES))
    for result in results:
        result.wait()

    for exchange, target, rows in (
        (FWD[0], first_fwd_in, 2), (BACK[0], back_in, 1), (FWD[1], fwd_in.at[0], 1),
        (BACK[1], last_back_in, 1), (FWD[2], fwd_in.at[1], 1), (LAST, last_in, 1), (SUMS, sum_in, 1),
    ):
        finish(exchange, target, rows).wait_send()
    for step in range(3):
        remote(core_out.at[step], core_in.at[step], CORE[step], partner).wait_send()


def finish_step(scaled, gradient, alphas, increment_out, gradient_out, a, b, c, d, sem):
    copies = [
        pltpu.make_async_copy(source, target, sem.at[i])
        for i, (source, target) in enumerate(
            ((alphas, c), (gradient, b), (scaled, a), (b, gradient_out), (d, increment_out))
        )
    ]
    for copy in copies[:3]:
        copy.start()
    copies[1].wait()
    copies[3].start()
    copies[0].wait()
    copies[2].wait()
    d[...] = -(a[...] + c[...] * b[...])
    copies[4].start()
    copies[3].wait()
    copies[4].wait()


def body(
    flux, prior_flux, prior_precision, obs_value, obs_weight, footprint, counts, obs_blocks,
    cell_blocks,
):
    cells = (256, LANES)
    message, double = (CHIPS, LANES), (2 * CHIPS, LANES)
    results = pl.pallas_call(
        kernel,
        out_shape=[jax.ShapeDtypeStruct(cells, F32)] * 2 + [jax.ShapeDtypeStruct((1, LANES), F32)],
        in_specs=[pl.BlockSpec(memory_space=pltpu.HBM)] * 9,
        out_specs=[pl.BlockSpec(memory_space=pltpu.HBM)] * 2 + [pl.BlockSpec(memory_space=pltpu.VMEM)],
        scratch_shapes=[
            pltpu.VMEM(cells, F32),
            pltpu.VMEM(cells, F32),
            pltpu.VMEM(cells, F32),
            pltpu.VMEM((LANES, LANES), F32),
            pltpu.VMEM((LANES, LANES), F32),
            pltpu.VMEM((1, REGIONS), jnp.int32),
            pltpu.VMEM((MOST, REGIONS), jnp.int32),
            pltpu.VMEM((MOST, REGIONS), jnp.int32),
            pltpu.VMEM((TILES * BLOCKS, LANES), F32),
            pltpu.VMEM((MOST * SHARE, BLOCK, LANES), F32),
            pltpu.VMEM((LANES, LANES), F32),
            pltpu.VMEM((BLOCK, CBLK), F32),
            pltpu.VMEM((BLOCK, CBLK), F32),
            pltpu.VMEM((BLOCK, CBLK), F32),
            pltpu.VMEM((BLOCK, BLOCKS), F32),
            pltpu.VMEM((BLOCK, BLOCKS), F32),
            pltpu.VMEM((BLOCK, BLOCKS), F32),
            pltpu.VMEM((CBLK, BLOCKS), BF16),
            pltpu.VMEM((BLOCKS, BLOCKS), BF16),
            pltpu.VMEM((MOST * LANES, OBLK), BF16),
            pltpu.VMEM((2, 2, BLOCK, LANES), F32),
            pltpu.VMEM(double, F32),
            pltpu.VMEM(double, F32),
            pltpu.VMEM((2, *message), F32),
            pltpu.VMEM((2, *message), F32),
            pltpu.VMEM(message, F32),
            pltpu.VMEM(message, F32),
            pltpu.VMEM(message, F32),
            pltpu.VMEM(message, F32),
            pltpu.VMEM((3, SHARE + 8, OBLK), F32),
            pltpu.VMEM((3, SHARE + 8, OBLK), F32),
            pltpu.VMEM((SHARE, OBLK), F32),
            pltpu.VMEM((1, LANES), F32),
            pltpu.VMEM(message, F32),
            pltpu.VMEM((1, LANES), F32),
            pltpu.VMEM(message, F32),
            pltpu.VMEM(cells, F32),
            pltpu.VMEM(cells, F32),
            pltpu.SemaphoreType.DMA((TILES,)),
            pltpu.SemaphoreType.DMA((8,)),
            pltpu.SemaphoreType.DMA((EXCHANGES,)),
            pltpu.SemaphoreType.DMA((EXCHANGES,)),
            pltpu.SemaphoreType.DMA((2,)),
        ],
        compiler_params=pltpu.CompilerParams(
            collective_id=0, has_side_effects=True, vmem_limit_bytes=60 * 1024 * 1024
        ),
        name="inversion",
    )(
        flux.reshape(cells),
        prior_flux.reshape(cells),
        prior_precision.reshape(cells),
        obs_value.reshape(LANES, LANES),
        obs_weight.reshape(LANES, LANES),
        footprint.reshape(BLOCKS, BLOCK * BLOCK),
        counts.reshape(1, REGIONS),
        obs_blocks.reshape(REGIONS, MOST).T,
        cell_blocks.reshape(REGIONS, MOST).T,
    )
    hbm = [pl.BlockSpec(memory_space=pltpu.HBM)]
    increment, gradient = pl.pallas_call(
        finish_step,
        out_shape=[jax.ShapeDtypeStruct(cells, F32)] * 2,
        in_specs=hbm * 3,
        out_specs=hbm * 2,
        scratch_shapes=[
            pltpu.VMEM(cells, F32),
            pltpu.VMEM(cells, F32),
            pltpu.VMEM((1, LANES), F32),
            pltpu.VMEM(cells, F32),
            pltpu.SemaphoreType.DMA((5,)),
        ],
        name="finish_step",
    )(*results)
    return increment.reshape(flux.shape), gradient.reshape(flux.shape)


def solution(mesh):
    placed = (
        P("slot", "region"),
        P("slot", "region"),
        P("slot", "region"),
        P("region"),
        P("region"),
        P("slot", "region", None, None, None),
        P("slot", "region", None),
        P("slot", "region", None, None),
        P("slot", "region", None, None),
    )
    return jax.shard_map(
        body,
        mesh=mesh,
        in_specs=placed,
        out_specs=(P("slot", "region"), P("slot", "region")),
        check_vma=False,
    )
```

```python
import jax
import jax.numpy as jnp
from jax import lax
from jax.experimental import pallas as pl
from jax.experimental.pallas import tpu as pltpu
from jax.sharding import PartitionSpec as P

REGIONS = 32
SLOTS = 8
MOST = 8
BLOCK = 64
BLOCKS = REGIONS * MOST
CBLK = 512
OBLK = 256
LANES = 128
CHIPS = 128
SHARE = 16
PAIRS = SHARE // 2
TILES = BLOCK // 2
MESH = pl.DeviceIdType.MESH
F32 = jnp.float32
BF16 = jnp.bfloat16
AS_IS = ((1,), (0,))
TURNED = ((1,), (1,))

FWD, BACK, LAST, CORE, PLANE, LINE = (0, 1, 2), (3, 4), 5, (6, 7, 8), 9, 10
EXCHANGES = 11


def hops(step):
    z, x, y = step
    return min(z, 8 - z) + min(x, 4 - x) + min(y, 4 - y)


STEPS = sorted(
    [(z, x, y) for z in range(8) for x in range(4) for y in range(4) if z or x or y],
    key=lambda step: (-hops(step), step),
)


def iota(shape, axis):
    return lax.broadcasted_iota(jnp.int32, shape, axis)


def pick(x, onehot, dims):
    high = x.astype(BF16)
    rest = x - high.astype(F32)
    middle = rest.astype(BF16)
    low = (rest - middle.astype(F32)).astype(BF16)
    pieces = jnp.concatenate([high, middle, low], axis=0)
    out = lax.dot_general(pieces, onehot, (dims, ((), ())), preferred_element_type=F32)
    rows = x.shape[0]
    return out[:rows] + out[rows : 2 * rows] + out[2 * rows :]


def load_cells(ref):
    x = ref[...]
    a, b = x[:LANES].T, x[LANES:].T
    return jnp.concatenate([a[:BLOCK], b[:BLOCK], a[BLOCK:], b[BLOCK:]], axis=1)


def store_cells(x):
    a = jnp.concatenate([x[:, :LANES], x[:, 2 * LANES : 3 * LANES]], axis=0).T
    b = jnp.concatenate([x[:, LANES : 2 * LANES], x[:, 3 * LANES :]], axis=0).T
    return jnp.concatenate([a, b], axis=0)


def total(x):
    return jnp.sum(jnp.sum(x, axis=0, keepdims=True), axis=1, keepdims=True)


def side_by_side(x):
    return jnp.concatenate([x[SHARE * k : SHARE * (k + 1)] for k in range(MOST)], axis=1)


def stacked(x):
    return jnp.concatenate([x[:, LANES * k : LANES * (k + 1)] for k in range(MOST)], axis=0)


def kernel(
    flux_hbm, prior_hbm, precision_hbm, value_hbm, weight_hbm, foot, counts_hbm, obs_hbm, cell_hbm,
    scaled_hbm, gradient_hbm, alphas,
    flux, prior, precision, value, weight, counts, obs_blocks, cell_blocks,
    foot_in, foot_t, part, cells, prec, pull, terms, found, pulled, onehot_c, meet, onehot_a, observed,
    first_fwd_out, first_fwd_in, fwd_out, fwd_in, back_out, back_in, last_back_out, last_back_in,
    core_out, core_in, first_image, plane_out, plane_in, line_out, line_in, last_out, last_in, scaled, gradient,
    foot_sem, in_sem, send_sem, recv_sem, out_sem,
):
    region, slot = lax.axis_index("region"), lax.axis_index("slot")
    y, core = lax.div(slot, 2), lax.rem(slot, 2)
    z, x = lax.div(region, 4), lax.rem(region, 4)
    me = y * REGIONS + region
    partner = {"slot": slot + 1 - 2 * core}
    at_z = [lax.rem(z + step, 8) * 4 for step in range(8)]
    at_x = [lax.rem(x + step, 4) for step in range(4)]
    at_y = [lax.rem(y + step, 4) for step in range(4)]
    slot_at = [at * 2 + core for at in at_y]
    row_at = [at * REGIONS for at in at_y]

    loads = [
        pltpu.make_async_copy(source, target, in_sem.at[i])
        for i, (source, target) in enumerate((
            (obs_hbm, obs_blocks), (cell_hbm, cell_blocks), (counts_hbm, counts), (flux_hbm, flux),
            (prior_hbm, prior), (precision_hbm, precision), (value_hbm, value), (weight_hbm, weight),
        ))
    ]

    def foot_copy(tile):
        return pltpu.make_async_copy(
            foot.at[:, pl.ds(tile * LANES, LANES)],
            foot_in.at[pl.ds(tile * BLOCKS, BLOCKS), :],
            foot_sem.at[tile],
        )

    starts = loads[:4] + [
        foot_copy(share * PAIRS + pair) for pair in range(PAIRS) for share in range(4)
    ] + loads[4:]
    barrier = pltpu.get_barrier_semaphore()
    for i, (dz, dx, dy) in enumerate(STEPS):
        pl.semaphore_signal(
            barrier, inc=1, device_id={"region": at_z[dz] + at_x[dx], "slot": slot_at[dy]},
            device_id_type=MESH,
        )
        if i % 2 == 1 and starts:
            starts.pop(0).start()
    pl.semaphore_signal(barrier, inc=1, device_id=partner, device_id_type=MESH)

    def remote(source, target, exchange, device):
        return pltpu.make_async_remote_copy(
            src_ref=source,
            dst_ref=target,
            send_sem=send_sem.at[exchange],
            recv_sem=recv_sem.at[exchange],
            device_id=device,
            device_id_type=MESH,
        )

    def send(exchange, source, target, rows=1):
        for dz, dx, dy in STEPS:
            there = at_z[dz] + at_x[dx]
            chip = row_at[dy] + there if source.shape[0] > 1 else 0
            remote(
                source.at[pl.ds(chip * rows, rows), :], target.at[pl.ds(me * rows, rows), :], exchange,
                {"region": there, "slot": slot_at[dy]},
            ).start()

    def finish(exchange, target, rows=1, count=CHIPS - 1):
        others = target.at[pl.ds(0, count * rows), :]
        return remote(others, others, exchange, partner)

    def keep(source, target, rows=1):
        target[pl.ds(me * rows, rows), :] = source[pl.ds(me * rows, rows), :]

    def every_other(first):
        return pl.ds(first, CHIPS, stride=2)

    lane = iota((REGIONS, BLOCKS), 1)
    of_region = lane % REGIONS == iota((REGIONS, BLOCKS), 0)
    of_place = iota((MOST, BLOCKS), 1) // REGIONS == iota((MOST, BLOCKS), 0)
    loads[1].wait()
    loads[2].wait()
    cell_index = jnp.dot(
        cell_blocks[...].astype(F32), of_region.astype(F32), precision=lax.Precision.HIGHEST,
        preferred_element_type=F32,
    )
    cell_index = jnp.sum(jnp.where(of_place, cell_index, 0.0), axis=0, keepdims=True)
    live = jnp.dot(
        counts[...].astype(F32), of_region.astype(F32), precision=lax.Precision.HIGHEST,
        preferred_element_type=F32,
    )
    live = (iota((1, BLOCKS), 1) // REGIONS).astype(F32) < live - 0.5
    cell_index = jnp.where(live, cell_index, -1.0)
    row = iota((CBLK, BLOCKS), 0)
    block = ((row % 256) * 2 + row // 256).astype(F32)
    onehot_c[...] = jnp.where(block == cell_index, 1.0, 0.0).astype(BF16)

    group = iota((1, LANES), 1) // REGIONS

    loads[3].wait()
    found[...] = pick(load_cells(flux), onehot_c[...], AS_IS)

    loads[0].wait()
    index = jnp.concatenate(
        [obs_blocks[...].astype(F32), jnp.zeros((MOST, LANES - REGIONS), F32)], axis=1
    )
    index = jnp.concatenate([index, jnp.zeros((LANES - MOST, LANES), F32)], axis=0).T
    index = jnp.concatenate([index[:REGIONS]] * 4, axis=0)
    first_fwd_out[every_other(1), :] = index

    for pair in range(PAIRS):
        for share in range(4):
            foot_copy(share * PAIRS + pair).wait()

        @pl.loop(0, MOST, unroll=MOST)
        def _(k):
            block = [
                foot_in[pl.ds((share * PAIRS + pair) * BLOCKS + k, REGIONS, stride=MOST), :]
                for share in range(4)
            ]
            block = jnp.concatenate(block, axis=0).T
            foot_t[pl.ds(k * SHARE + 2 * pair, 2)] = block.reshape(2, BLOCK, LANES)

    low = [iota((8, LANES), 0) // shift % 2 == 0 for shift in (1, 2, 4)]

    def partials(picked):
        rows = []
        for k in range(MOST):
            field = picked[:, k // 4 * LANES : (k // 4 + 1) * LANES]
            field = jnp.where(group == k % 4, field, 0.0)
            field = field + pltpu.roll(field, 2 * REGIONS, 1)
            field = field + pltpu.roll(field, REGIONS, 1)
            for start in range(0, SHARE, 8):
                sums = []
                for i in range(start, start + 8):
                    acc = foot_t[k * SHARE + i, :8, :] * field[:8]
                    for c in range(8, BLOCK, 8):
                        acc = acc + foot_t[k * SHARE + i, c : c + 8, :] * field[c : c + 8]
                    sums.append(acc)
                for mask, shift in zip(low, (1, 2, 4)):
                    sums = [
                        jnp.where(mask, a, b) + pltpu.roll(jnp.where(mask, b, a), 8 - shift, 0)
                        for a, b in zip(sums[::2], sums[1::2])
                    ]
                rows += sums
        return jnp.concatenate(rows, axis=0).T

    def summed(came, step, numer, denom):
        dense = pick(side_by_side(came.T), onehot_a[...], AS_IS)
        scalars = jnp.where(iota((8, OBLK), 1) < LANES, numer, denom)
        core_out[step] = jnp.concatenate([dense, scalars], axis=0)
        copy = remote(core_out.at[step], core_in.at[step], CORE[step], partner)
        copy.start()
        copy.wait_recv()
        both = core_out[step] + core_in[step]
        scalars = both[SHARE : SHARE + 1]
        return both[:SHARE], scalars[:, :1], scalars[:, LANES : LANES + 1]

    def to_sources(weighted):
        return stacked(pick(weighted, onehot_a[...], TURNED)).T

    def adjoint(came):
        part[...] = came.T
        halves = []
        for half in range(2):
            merged = jnp.zeros((BLOCK, LANES), F32)
            for place in range(4):
                k = half * 4 + place
                acc = foot_t[k * SHARE] * part[k * SHARE : k * SHARE + 1, :]
                for i in range(1, SHARE):
                    at = k * SHARE + i
                    acc = acc + foot_t[at] * part[at : at + 1, :]
                acc = acc + pltpu.roll(acc, 2 * REGIONS, 1)
                acc = acc + pltpu.roll(acc, REGIONS, 1)
                merged = jnp.where(group == place, acc, merged)
            halves.append(merged)
        return jnp.concatenate(halves, axis=1)

    left = iota((1, LANES), 1) < LANES // 2

    def ratio(rows):
        scalars = jnp.sum(rows, axis=0, keepdims=True)
        return scalars[:, :1] / scalars[:, LANES // 2 : LANES // 2 + 1]

    first_fwd_out[every_other(0), :] = partials(found[...])
    keep(first_fwd_out, first_fwd_in, 2)
    pl.semaphore_wait(barrier, CHIPS)
    send(FWD[0], first_fwd_out, first_fwd_in, 2)
    for load in loads[4:]:
        load.wait()
    prec[...] = load_cells(precision)
    pull[...] = prec[...] * (load_cells(flux) - load_cells(prior))
    pulled[...] = pick(pull[...], onehot_c[...], AS_IS)
    meet[...] = lax.dot_general(
        onehot_c[...], onehot_c[...], (((0,), (0,)), ((), ())), preferred_element_type=F32
    ).astype(BF16)
    observed[0] = value[...].T.reshape(2, BLOCK, LANES)
    observed[1] = weight[...].T.reshape(2, BLOCK, LANES)
    mine = pl.ds(pl.multiple_of(y * SHARE, SHARE), SHARE)
    seen = jnp.concatenate([observed[0, 0, mine, :], observed[0, 1, mine, :]], axis=1)
    weights = jnp.concatenate([observed[1, 0, mine, :], observed[1, 1, mine, :]], axis=1)
    finish(FWD[0], first_fwd_in, 2).wait_recv()
    index = first_fwd_in[every_other(1), :]
    column = iota((LANES, OBLK), 1)
    block = ((column % LANES) * 2 + column // LANES).astype(F32)
    for k in range(MOST):
        onehot_a[k * LANES : (k + 1) * LANES, :] = jnp.where(
            index[:, k : k + 1] == block, 1.0, 0.0
        ).astype(BF16)
    image, _, _ = summed(first_fwd_in[every_other(0), :], 0, 0.0, 0.0)
    back_out[...] = to_sources(weights * (image - seen))
    keep(back_out, back_in)
    send(BACK[0], back_out, back_in)
    finish(BACK[0], back_in).wait_recv()

    term = adjoint(back_in[...])
    terms[...] = term
    picked = pick(term, meet[...], AS_IS) + pulled[...]
    fwd_out[0] = partials(picked)
    keep(fwd_out.at[0], fwd_in.at[0])
    send(FWD[1], fwd_out.at[0], fwd_in.at[0])
    first = pick(terms[...], onehot_c[...], TURNED) + pull[...]
    cells[...] = first
    pulled[...] = pick(prec[...] * first, onehot_c[...], AS_IS)
    scaled[...] = store_cells(first)
    square = first * first
    numer, denom = total(square), total(prec[...] * square)
    finish(FWD[1], fwd_in.at[0]).wait_recv()
    image, numer, denom = summed(fwd_in[0], 1, numer, denom)
    first_image[...] = image
    weighted = weights * image
    last_back_out[...] = to_sources(weighted)
    keep(last_back_out, last_back_in)
    send(BACK[1], last_back_out, last_back_in)
    plane_out[...] = jnp.where(left, numer, denom + total(weighted * image))
    plane_in[pl.ds(y * 4 + x, 1), :] = plane_out[...]
    for dz, dx, dy in STEPS:
        if dz == 0:
            remote(
                plane_out, plane_in.at[pl.ds(y * 4 + x, 1), :], PLANE,
                {"region": at_z[0] + at_x[dx], "slot": slot_at[dy]},
            ).start()
    finish(BACK[1], last_back_in).wait_recv()

    term = adjoint(last_back_in[...])
    terms[...] = term
    picked = pick(term, meet[...], AS_IS) + pulled[...]
    fwd_out[1] = partials(picked)
    keep(fwd_out.at[1], fwd_in.at[1])
    send(FWD[2], fwd_out.at[1], fwd_in.at[1])
    finish(PLANE, plane_in, count=15).wait_recv()
    line_out[...] = jnp.sum(plane_in[...], axis=0, keepdims=True)
    line_in[pl.ds(z, 1), :] = line_out[...]
    for dz in (4, 3, 5, 2, 6, 1, 7):
        remote(
            line_out, line_in.at[pl.ds(z, 1), :], LINE, {"region": at_z[dz] + at_x[0], "slot": slot}
        ).start()
    finish(LINE, line_in, count=7).wait_recv()
    alpha = ratio(line_in[...])
    first = cells[...]
    second = first - alpha * (pick(terms[...], onehot_c[...], TURNED) + prec[...] * first)
    gradient[...] = store_cells(second)
    scaled[...] = scaled[...] * alpha
    results = [
        pltpu.make_async_copy(gradient, gradient_hbm, out_sem.at[0]),
        pltpu.make_async_copy(scaled, scaled_hbm, out_sem.at[1]),
    ]
    for result in results:
        result.start()
    square = second * second
    numer, denom = total(square), total(prec[...] * square)
    finish(FWD[2], fwd_in.at[1]).wait_recv()
    image, numer, denom = summed(fwd_in[1], 2, numer, denom)
    image = first_image[...] - alpha * image
    last_out[...] = jnp.where(left, numer, denom + total(weights * image * image))
    last_in[pl.ds(me, 1), :] = last_out[...]
    send(LAST, last_out, last_in)
    finish(LAST, last_in).wait_recv()
    alphas[...] = jnp.broadcast_to(ratio(last_in[...]), (1, LANES))
    for result in results:
        result.wait()

    for exchange, target, rows in (
        (FWD[0], first_fwd_in, 2), (BACK[0], back_in, 1), (FWD[1], fwd_in.at[0], 1),
        (BACK[1], last_back_in, 1), (FWD[2], fwd_in.at[1], 1), (LAST, last_in, 1),
    ):
        finish(exchange, target, rows).wait_send()
    finish(PLANE, plane_in, count=15).wait_send()
    finish(LINE, line_in, count=7).wait_send()
    for step in range(3):
        remote(core_out.at[step], core_in.at[step], CORE[step], partner).wait_send()


def finish_step(scaled, gradient, alphas, increment_out, gradient_out, a, b, c, d, sem):
    copies = [
        pltpu.make_async_copy(source, target, sem.at[i])
        for i, (source, target) in enumerate(
            ((alphas, c), (gradient, b), (scaled, a), (b, gradient_out), (d, increment_out))
        )
    ]
    for copy in copies[:3]:
        copy.start()
    copies[1].wait()
    copies[3].start()
    copies[0].wait()
    copies[2].wait()
    d[...] = -(a[...] + c[...] * b[...])
    copies[4].start()
    copies[3].wait()
    copies[4].wait()


def body(
    flux, prior_flux, prior_precision, obs_value, obs_weight, footprint, counts, obs_blocks,
    cell_blocks,
):
    cells = (256, LANES)
    message, double = (CHIPS, LANES), (2 * CHIPS, LANES)
    results = pl.pallas_call(
        kernel,
        out_shape=[jax.ShapeDtypeStruct(cells, F32)] * 2 + [jax.ShapeDtypeStruct((1, LANES), F32)],
        in_specs=[pl.BlockSpec(memory_space=pltpu.HBM)] * 9,
        out_specs=[pl.BlockSpec(memory_space=pltpu.HBM)] * 2 + [pl.BlockSpec(memory_space=pltpu.VMEM)],
        scratch_shapes=[
            pltpu.VMEM(cells, F32),
            pltpu.VMEM(cells, F32),
            pltpu.VMEM(cells, F32),
            pltpu.VMEM((LANES, LANES), F32),
            pltpu.VMEM((LANES, LANES), F32),
            pltpu.VMEM((1, REGIONS), jnp.int32),
            pltpu.VMEM((MOST, REGIONS), jnp.int32),
            pltpu.VMEM((MOST, REGIONS), jnp.int32),
            pltpu.VMEM((TILES * BLOCKS, LANES), F32),
            pltpu.VMEM((MOST * SHARE, BLOCK, LANES), F32),
            pltpu.VMEM((LANES, LANES), F32),
            pltpu.VMEM((BLOCK, CBLK), F32),
            pltpu.VMEM((BLOCK, CBLK), F32),
            pltpu.VMEM((BLOCK, CBLK), F32),
            pltpu.VMEM((BLOCK, BLOCKS), F32),
            pltpu.VMEM((BLOCK, BLOCKS), F32),
            pltpu.VMEM((BLOCK, BLOCKS), F32),
            pltpu.VMEM((CBLK, BLOCKS), BF16),
            pltpu.VMEM((BLOCKS, BLOCKS), BF16),
            pltpu.VMEM((MOST * LANES, OBLK), BF16),
            pltpu.VMEM((2, 2, BLOCK, LANES), F32),
            pltpu.VMEM(double, F32),
            pltpu.VMEM(double, F32),
            pltpu.VMEM((2, *message), F32),
            pltpu.VMEM((2, *message), F32),
            pltpu.VMEM(message, F32),
            pltpu.VMEM(message, F32),
            pltpu.VMEM(message, F32),
            pltpu.VMEM(message, F32),
            pltpu.VMEM((3, SHARE + 8, OBLK), F32),
            pltpu.VMEM((3, SHARE + 8, OBLK), F32),
            pltpu.VMEM((SHARE, OBLK), F32),
            pltpu.VMEM((1, LANES), F32),
            pltpu.VMEM((16, LANES), F32),
            pltpu.VMEM((1, LANES), F32),
            pltpu.VMEM((8, LANES), F32),
            pltpu.VMEM((1, LANES), F32),
            pltpu.VMEM(message, F32),
            pltpu.VMEM(cells, F32),
            pltpu.VMEM(cells, F32),
            pltpu.SemaphoreType.DMA((TILES,)),
            pltpu.SemaphoreType.DMA((8,)),
            pltpu.SemaphoreType.DMA((EXCHANGES,)),
            pltpu.SemaphoreType.DMA((EXCHANGES,)),
            pltpu.SemaphoreType.DMA((2,)),
        ],
        compiler_params=pltpu.CompilerParams(
            collective_id=0, has_side_effects=True, vmem_limit_bytes=60 * 1024 * 1024
        ),
        name="inversion",
    )(
        flux.reshape(cells),
        prior_flux.reshape(cells),
        prior_precision.reshape(cells),
        obs_value.reshape(LANES, LANES),
        obs_weight.reshape(LANES, LANES),
        footprint.reshape(BLOCKS, BLOCK * BLOCK),
        counts.reshape(1, REGIONS),
        obs_blocks.reshape(REGIONS, MOST).T,
        cell_blocks.reshape(REGIONS, MOST).T,
    )
    hbm = [pl.BlockSpec(memory_space=pltpu.HBM)]
    increment, gradient = pl.pallas_call(
        finish_step,
        out_shape=[jax.ShapeDtypeStruct(cells, F32)] * 2,
        in_specs=hbm * 3,
        out_specs=hbm * 2,
        scratch_shapes=[
            pltpu.VMEM(cells, F32),
            pltpu.VMEM(cells, F32),
            pltpu.VMEM((1, LANES), F32),
            pltpu.VMEM(cells, F32),
            pltpu.SemaphoreType.DMA((5,)),
        ],
        name="finish_step",
    )(*results)
    return increment.reshape(flux.shape), gradient.reshape(flux.shape)


def solution(mesh):
    placed = (
        P("slot", "region"),
        P("slot", "region"),
        P("slot", "region"),
        P("region"),
        P("region"),
        P("slot", "region", None, None, None),
        P("slot", "region", None),
        P("slot", "region", None, None),
        P("slot", "region", None, None),
    )
    return jax.shard_map(
        body,
        mesh=mesh,
        in_specs=placed,
        out_specs=(P("slot", "region"), P("slot", "region")),
        check_vma=False,
    )
```
